512 devices in a mesh: layer: 32 (over y, x), space: 16 (over z, core).
Axes of the slice: x: 4, y: 8, z: 8, core: 2. Of those that a mesh axis runs over, the one named last changes fastest.
Arguments:
- images: float32 [4, 32, 32, 128], P(None, 'space'), may hold values from -6 to 6
- end_guess: float32 [32, 4, 32, 32, 128], P('layer', None, 'space'), may hold values from -6 to 6
- end_adjoint: float32 [32, 4, 32, 32, 128], P('layer', None, 'space'), may hold values from -6 to 6
- weights: bfloat16 [128, 1152, 128], P('layer'), may hold values from -0.1875 to 0.1875
Outputs:
- section_ends: float32 [32, 4, 32, 32, 128], P('layer', None, 'space')
- start_adjoint: float32 [32, 4, 32, 32, 128], P('layer', None, 'space')
- weight_grad: float32 [128, 1152, 128], P('layer', 'space')
The draws below stay inside these ranges and needn't reach their ends.
All inputs are finite; a program needn't handle non-finite values.
Results may differ from the reference program's by a relative error of at most 0.0065.
Values may be sent and summed in bfloat16 or wider, within the bound.
No kernel may reach another device: no remote copies, remote signals or barrier semaphores. Data moves between devices by JAX's collectives and lax.ppermute only.
A program may use at most 64 MiB of HBM per device.

```python
import jax
import jax.numpy as jnp
from jax import lax

C = 128
HEIGHT = 32
WIDTH = 32
SECTION = 4
IMAGES = 4
SECTIONS = 32
LAYERS = 128


def levels(rng, shape, cuts, least, high):
    factor_of, own = 1.0, jax.random.fold_in(rng, 6)
    for position, blocks in cuts:
        heights = jnp.exp(jax.random.uniform(jax.random.fold_in(own, position), (blocks,), jnp.float32, least / len(cuts), high / len(cuts)))
        factor_of = factor_of * jnp.repeat(heights, shape[position] // blocks).reshape([-1 if axis == position else 1 for axis in range(len(shape))])
    return factor_of


def normal_values(own_key, shape, scale, limit, cuts=(), held_as=jnp.bfloat16):
    entries = scale * jax.random.normal(own_key, shape, jnp.float32)
    if cuts:
        entries = entries * levels(own_key, shape, cuts, -0.22, 0.18)
    return jnp.clip(entries, -limit, limit).astype(held_as)


def setup_inputs(seed: int = 0) -> dict:
    arg_keys = jax.random.split(jax.random.key(seed), 5)
    images = normal_values(arg_keys[0], (IMAGES, HEIGHT, WIDTH, C), 1.0, 6.0, ((1, 16),), jnp.float32)
    end_guess = normal_values(arg_keys[1], (SECTIONS, IMAGES, HEIGHT, WIDTH, C), 1.0, 6.0, ((0, 32), (2, 16)), jnp.float32)
    end_adjoint = normal_values(arg_keys[2], (SECTIONS, IMAGES, HEIGHT, WIDTH, C), 1.0, 6.0, ((0, 32), (2, 16)), jnp.float32)
    weights = normal_values(arg_keys[3], (LAYERS, 9 * C, C), (9 * C) ** -0.5, 0.1875, ((0, 32),))
    return dict(images=images, end_guess=end_guess, end_adjoint=end_adjoint, weights=weights)


STEP_SIZE = 0.1


def patches(extended, margin, amount, direction):
    image_width = extended.shape[2]
    channels = extended.shape[3]
    padded = jnp.pad(extended, ((0, 0), (0, 0), (1, 1), (0, 0)))
    pieces = []
    for offset in range(9):
        row_shift = direction * (offset // 3 - 1)
        col_shift = direction * (offset % 3 - 1)
        pieces.append(padded[:, margin + row_shift: margin + row_shift + amount, 1 + col_shift: 1 + col_shift + image_width])
    return jnp.concatenate(pieces, axis=-1).reshape(extended.shape[0] * amount * image_width, 9 * channels)


def activation(states):
    return jnp.tanh(states).astype(jnp.bfloat16)


def flip_kernel(kernel):
    channels = kernel.shape[1]
    return kernel.reshape(9, channels, channels).transpose(0, 2, 1).reshape(9 * channels, channels)


def convolve(active, kernel, direction):
    extended = jnp.pad(active, ((0, 0), (1, 1), (0, 0), (0, 0)))
    columns = patches(extended, 1, active.shape[1], direction)
    result = jnp.dot(columns, kernel, preferred_element_type=jnp.float32)
    return result.reshape(active.shape[0], active.shape[1], active.shape[2], kernel.shape[1])


def apply_couple(couple):
    return convolve(activation(couple[0]), couple[1], 1)


def conv_all(states, kernels):
    return lax.map(apply_couple, (states, kernels))


def weight_term(couple):
    active, adjoint_low = couple
    extended = jnp.pad(active, ((0, 0), (1, 1), (0, 0), (0, 0)))
    columns = patches(extended, 1, active.shape[1], 1)
    flat_adjoint = adjoint_low.reshape(-1, adjoint_low.shape[3])
    return STEP_SIZE * lax.dot_general(columns, flat_adjoint, (((0,), (0,)), ((), ())), preferred_element_type=jnp.float32)


def back_couple(couple):
    return convolve(couple[0], flip_kernel(couple[1]), -1)


def reference(images, end_guess, end_adjoint, weights):
    sections = end_guess.shape[0]
    channels = weights.shape[2]
    kernels = weights.reshape(sections, SECTION, 9 * channels, channels)
    leading = kernels[:, 0]

    def starts(ends):
        return jnp.concatenate([images[None], ends[:-1]], axis=0)

    def fine_run(begin_states, amount):
        states = [begin_states]
        first_term = None
        for segment_index in range(amount):
            result = conv_all(states[-1], kernels[:, segment_index])
            if segment_index == 0:
                first_term = result
            states.append(states[-1] + STEP_SIZE * result)
        return states, first_term

    def level_round(level_values, segment_index):
        received = starts(level_values)[segment_index::4]
        return received + SECTION * STEP_SIZE * conv_all(received, leading[segment_index::4]) + defect[segment_index::4]

    relaxed = fine_run(starts(end_guess), SECTION)[0][-1]
    begin_states = starts(relaxed)
    states, first_term = fine_run(begin_states, SECTION)
    defect = states[-1] - (begin_states + SECTION * STEP_SIZE * first_term)
    level_values = relaxed.at[0::4].set(states[-1][0::4])
    for segment_index in (1, 2):
        level_values = level_values.at[segment_index::4].set(level_round(level_values, segment_index))
    closing = level_round(level_values, 3)
    coarse_kernels = leading[3::4]
    long_step = 4 * SECTION * STEP_SIZE
    group_begin = begin_states[0::4]
    defect_two = closing - (group_begin + long_step * conv_all(group_begin, coarse_kernels))
    coarse_value = images
    coarse_list = []
    for group_index in range(sections // 4):
        coarse_value = coarse_value + long_step * convolve(activation(coarse_value), coarse_kernels[group_index], 1) + defect_two[group_index]
        coarse_list.append(coarse_value)
    level_values = level_values.at[3::4].set(jnp.stack(coarse_list))
    for segment_index in (0, 1, 2):
        level_values = level_values.at[segment_index::4].set(level_round(level_values, segment_index))
    section_ends = level_values
    final_states = fine_run(starts(section_ends), SECTION - 1)[0]
    adjoint = end_adjoint
    grad_list = [None] * SECTION
    for segment_index in reversed(range(SECTION)):
        slopes = jnp.tanh(final_states[segment_index])
        active = slopes.astype(jnp.bfloat16)
        adjoint_low = adjoint.astype(jnp.bfloat16)
        grad_list[segment_index] = lax.map(weight_term, (active, adjoint_low))
        back_term = lax.map(back_couple, (adjoint_low, kernels[:, segment_index]))
        adjoint = adjoint + STEP_SIZE * (1.0 - slopes * slopes) * back_term
    weight_grad = jnp.stack(grad_list, axis=1).reshape(sections * SECTION, 9 * channels, channels)
    return section_ends, adjoint, weight_grad
```

```python
import jax
import jax.numpy as jnp
from jax import lax
from jax.experimental import pallas as pl
from jax.experimental.pallas import tpu as pltpu
from jax.sharding import PartitionSpec as P

STEP_SIZE = 0.1
SECTION = 4
SIDE = 32
CHANNELS = 128
PIXELS = SIDE * SIDE
PADDED = PIXELS + 2 * SIDE
PIECE = 128
CHUNK = 256
LOW = jnp.bfloat16
FULL = jnp.float32
SENT = jnp.float16

IMAGE = (PIXELS, CHANNELS)
PAD_SCRATCH = (PADDED, 3 * CHANNELS)


def clear(pad):
    edge = jnp.zeros((SIDE, 3 * CHANNELS), LOW)
    pad[0:SIDE, :] = edge
    pad[SIDE + PIXELS : PADDED, :] = edge


def put(pad, piece, values):
    column = lax.broadcasted_iota(jnp.int32, values.shape, 0) % SIDE
    left = jnp.where(column == 0, 0.0, pltpu.roll(values, 1, 0))
    right = jnp.where(column == SIDE - 1, 0.0, pltpu.roll(values, PIECE - 1, 0))
    rows = pl.ds(SIDE + piece * PIECE, PIECE)
    pad[rows, 0:CHANNELS] = left.astype(LOW)
    pad[rows, CHANNELS : 2 * CHANNELS] = values.astype(LOW)
    pad[rows, 2 * CHANNELS : 3 * CHANNELS] = right.astype(LOW)


def put_active(pad, state):
    for piece in range(PIXELS // PIECE):
        put(pad, piece, jnp.tanh(state[pl.ds(piece * PIECE, PIECE), :]))


def conv(pad, kernel, chunk):
    columns = jnp.concatenate(
        [pad[pl.ds(chunk * CHUNK + SIDE * shift, CHUNK), :] for shift in range(3)], axis=1
    )
    return jnp.dot(columns, kernel[...], preferred_element_type=FULL)


def chunks():
    return [(chunk, pl.ds(chunk * CHUNK, CHUNK)) for chunk in range(PIXELS // CHUNK)]


def relax_kernel(begin, weights, out, state, pad):
    clear(pad)
    state[...] = begin[...]

    def step(layer, carry):
        put_active(pad, state)
        for chunk, rows in chunks():
            state[rows, :] += STEP_SIZE * conv(pad, weights.at[layer], chunk)
        return carry

    lax.fori_loop(0, SECTION, step, 0)
    out[...] = state[...]


def fine_kernel(place, own, received, weights, closing, defect_out, send_out, state, base, first, pad):
    section, phase = place[0], place[1]
    clear(pad)
    for _, rows in chunks():
        begin = jnp.where(section == 0, own[rows, :], received[rows, :])
        state[rows, :] = begin
        base[rows, :] = begin

    put_active(pad, state)
    for chunk, rows in chunks():
        term = conv(pad, weights.at[0], chunk)
        first[rows, :] = term
        state[rows, :] += STEP_SIZE * term

    @pl.when(phase == 0)
    def _():
        for chunk, rows in chunks():
            long_term = (4 * SECTION * STEP_SIZE) * conv(pad, closing.at[SECTION - 1], chunk)
            base[rows, :] += long_term

    def step(layer, carry):
        put_active(pad, state)
        for chunk, rows in chunks():
            state[rows, :] += STEP_SIZE * conv(pad, weights.at[layer], chunk)
        return carry

    lax.fori_loop(1, SECTION, step, 0)
    for _, rows in chunks():
        begin = jnp.where(section == 0, own[rows, :], received[rows, :])
        last = state[rows, :]
        defect = (last - begin) - SECTION * STEP_SIZE * first[rows, :]
        defect_out[rows, :] = defect.astype(LOW)
        send_out[0, rows, :] = jnp.where(phase == 0, last, defect)
        total = jnp.where(section == 0, begin, last - base[rows, :])
        send_out[1, rows, :] = jnp.where(phase == 0, total, defect)


def first_round_kernel(place, sent, received, leading, out, state, pad):
    phase, in_first_group = place[1], place[0] < 4

    @pl.when(phase < 2)
    def _():
        clear(pad)
        for _, rows in chunks():
            state[rows, :] = jnp.where(phase == 0, sent[0, rows, :], received[0, rows, :])
        put_active(pad, state)
        for chunk, rows in chunks():
            defect = jnp.where(phase == 0, received[0, rows, :], sent[0, rows, :])
            total = jnp.where(phase == 0, sent[1, rows, :], received[1, rows, :])
            change = SECTION * STEP_SIZE * conv(pad, leading.at[1], chunk) + defect
            out[0, rows, :] = state[rows, :] + change
            out[1, rows, :] = total + jnp.where(in_first_group, 0.0, change)

    @pl.when(phase >= 2)
    def _():
        for _, rows in chunks():
            out[0, rows, :] = jnp.where(phase == 2, sent[0, rows, :], received[0, rows, :])
            out[1, rows, :] = jnp.where(phase == 2, received[0, rows, :], sent[0, rows, :])


def closing_kernel(place, sent, received, leading, out, total, state, pad):
    phase, in_first_group = place[1], place[0] < 4
    clear(pad)
    for _, rows in chunks():
        state[rows, :] = jnp.where(phase < 2, sent[0, rows, :], received[0, rows, :])
        total[rows, :] = jnp.where(phase < 2, sent[1, rows, :], received[1, rows, :])

    def step(turn, carry):
        put_active(pad, state)
        for chunk, rows in chunks():
            defect = jnp.where(phase < 2, received[turn, rows, :], sent[turn, rows, :])
            change = SECTION * STEP_SIZE * conv(pad, leading.at[2 + turn], chunk) + defect
            state[rows, :] += change
            total[rows, :] += jnp.where(in_first_group, 0.0, change)
        return carry

    lax.fori_loop(0, 2, step, 0)
    for _, rows in chunks():
        out[rows, :] = jnp.where(in_first_group, state[rows, :], total[rows, :])


def chain_kernel(place, images, received, mine, near, far, coarse, before_out, own_out, last_out, pad):
    state = last_out
    section, use_received, turn_of = place[0], place[2], place[3]
    clear(pad)
    for _, rows in chunks():
        state[rows, :] = jnp.where(use_received == 1, received[rows, :], 0.0)

    def step(turn, carry):
        @pl.when(turn == turn_of)
        def _():
            for _, rows in chunks():
                before_out[rows, :] = jnp.where(section < 4, images[rows, :], state[rows, :])

        put_active(pad, state)
        same_pair = turn // 2 == turn_of // 2
        same_place = turn % 2 == turn_of % 2
        place_in_pair = jnp.where(same_place, 0, 1)
        for chunk, rows in chunks():
            defect = jnp.where(same_place, mine[rows, :], near[rows, :])
            defect = jnp.where(same_pair, defect, far[place_in_pair, rows, :])
            state[rows, :] += (4 * SECTION * STEP_SIZE) * conv(pad, coarse.at[turn], chunk) + defect

        @pl.when(turn == turn_of)
        def _():
            own_out[...] = state[...]

        return carry

    lax.fori_loop(0, 4, step, 0)


def final_kernel(
    place, before, own, defects, leading, weights, flipped, end_adjoint,
    ends_out, grad_out,
    state, begin, end, slopes, change, pads, back_pad, grads,
):
    phase, replica = place[1], place[4]
    clear(back_pad)
    for layer in range(SECTION):
        clear(pads.at[layer])
    state[...] = before[...]
    begin[...] = before[...]
    end[...] = own[...]

    def level_step(turn, carry):
        put_active(back_pad, state)
        for chunk, rows in chunks():
            state[rows, :] += (
                SECTION * STEP_SIZE * conv(back_pad, leading.at[turn], chunk)
                + defects[turn, rows, :].astype(FULL)
            )

        @pl.when(phase == turn)
        def _():
            end[...] = state[...]

        @pl.when(phase == turn + 1)
        def _():
            begin[...] = state[...]

        return carry

    lax.fori_loop(0, 3, level_step, 0)

    def active(layer):
        for piece in range(PIXELS // PIECE):
            rows = pl.ds(piece * PIECE, PIECE)
            slope = jnp.tanh(begin[rows, :])
            slopes[layer, rows, :] = STEP_SIZE * (1.0 - slope * slope)
            put(pads.at[layer], piece, slope)

    def forward(layer, carry):
        active(layer)
        for chunk, rows in chunks():
            begin[rows, :] += STEP_SIZE * conv(pads.at[layer], weights.at[layer], chunk)
        return carry

    lax.fori_loop(0, SECTION - 1, forward, 0)
    active(SECTION - 1)
    change[...] = jnp.zeros(IMAGE, FULL)

    def backward(turn, carry):
        layer = SECTION - 1 - turn
        for piece in range(PIXELS // PIECE):
            rows = pl.ds(piece * PIECE, PIECE)
            put(back_pad, piece, end_adjoint[rows, :] + change[rows, :])
        low = back_pad[pl.ds(SIDE, PIXELS), CHANNELS : 2 * CHANNELS]
        for part in range(3):
            offset = 2 * replica + part
            columns = pads[
                layer,
                pl.ds(pl.multiple_of(SIDE * (offset // 3), SIDE), PIXELS),
                pl.ds(pl.multiple_of(CHANNELS * (offset % 3), CHANNELS), CHANNELS),
            ]
            grads[pl.ds(part * CHANNELS, CHANNELS), :] = STEP_SIZE * lax.dot_general(
                columns, low, (((0,), (0,)), ((), ())), preferred_element_type=FULL
            )
        grad_out[layer] = grads[pl.ds(pl.multiple_of(SIDE * replica, SIDE), 288), :].astype(LOW)
        for chunk, rows in chunks():
            change[rows, :] += slopes[layer, rows, :] * conv(back_pad, flipped.at[layer], chunk)
        return carry

    lax.fori_loop(0, SECTION, backward, 0)
    kept = pl.ds(pl.multiple_of(replica * 256, 256), 256)
    high = end[kept, :].astype(LOW)
    ends_out[0] = high
    ends_out[1] = (end[kept, :] - high.astype(FULL)).astype(LOW)
    ends_out[2] = change[kept, :].astype(LOW)


def call(body, outs, scratch, megabytes, place, *operands):
    held = pl.BlockSpec(memory_space=pltpu.VMEM)
    in_specs = [held] * len(operands)
    if place is not None:
        in_specs = [pl.BlockSpec(memory_space=pltpu.SMEM)] + in_specs
        operands = (place,) + operands
    return pl.pallas_call(
        body,
        out_shape=outs,
        in_specs=in_specs,
        out_specs=jax.tree.map(lambda _: held, outs),
        scratch_shapes=scratch,
        compiler_params=pltpu.CompilerParams(vmem_limit_bytes=megabytes * 1024 * 1024),
    )(*operands)


def shape(*dims, dtype=FULL):
    return jax.ShapeDtypeStruct(dims, dtype)


def wide():
    return pltpu.VMEM(IMAGE, FULL)


def padding():
    return pltpu.VMEM(PAD_SCRATCH, LOW)


def swap(block, distance, sections):
    moved = lax.ppermute(block.astype(SENT), "layer", [(i, i ^ distance) for i in range(sections)])
    return moved.astype(block.dtype)


def shift(block, distance, sections):
    route = [(i, i + distance) for i in range(sections - distance)]
    return lax.ppermute(block.astype(SENT), "layer", route).astype(block.dtype)


def local(images, end_guess, end_adjoint, weights):
    section = lax.axis_index("layer")
    tile = lax.axis_index("space")
    sections = lax.axis_size("layer")
    tiles = lax.axis_size("space")
    replica = tile // 4
    group = section // 4
    place = jnp.stack([section, section % 4, jnp.int32(0), group % 4, replica]).astype(jnp.int32)
    place_later = place.at[2].set(jnp.where(section >= 16, 1, 0))
    rows_of_groups = [[4 * g + i for i in range(4)] for g in range(sections // 4)]
    quads = [[16 * q + 4 * i + j for i in range(4)] for q in range(sections // 16) for j in range(4)]

    guess = jnp.where(section == 0, images, shift(end_guess[0], 1, sections))
    both = jnp.stack([guess, end_adjoint[0]], axis=1).astype(SENT)
    both = lax.all_to_all(jnp.tile(both, (tiles // 4, 1, 1, 1, 1)), "space", 0, 0, tiled=True)
    both = both.astype(FULL)
    start, adjoint_whole = both[:, 0].reshape(IMAGE), both[:, 1].reshape(IMAGE)

    leading = lax.all_gather(weights[0], "layer", axis_index_groups=rows_of_groups)
    flipped = (
        weights.reshape(SECTION, 9, CHANNELS, CHANNELS)[:, ::-1]
        .transpose(0, 1, 3, 2)
        .reshape(SECTION, 9 * CHANNELS, CHANNELS)
    )
    image_shape, pair_shape = shape(*IMAGE), shape(2, *IMAGE)

    relaxed = call(relax_kernel, image_shape, [wide(), padding()], 8, None, start, weights)
    received = shift(relaxed, 1, sections)
    closing_weights, _ = lax.optimization_barrier((leading[3], relaxed))
    coarse = lax.all_gather(closing_weights, "layer", axis_index_groups=quads)
    defect, send = call(
        fine_kernel,
        (shape(*IMAGE, dtype=LOW), pair_shape),
        [wide(), wide(), wide(), padding()],
        12, place, start, received, weights, leading,
    )
    defects = lax.all_gather(defect, "layer", axis_index_groups=rows_of_groups)
    received = swap(send, 1, sections)
    send = call(first_round_kernel, pair_shape, [wide(), padding()], 10, place, send, received, leading)
    received = swap(send, 2, sections)
    defect_two, base = call(
        closing_kernel, (image_shape, image_shape), [wide(), padding()], 10, place, send, received, leading
    )
    mine = defect_two.astype(SENT)
    near = lax.ppermute(mine, "layer", [(i, i ^ 4) for i in range(sections)])
    far = swap(jnp.stack([mine, near]), 8, sections).astype(FULL)
    near = near.astype(FULL)

    def chain(where, start_value):
        return call(
            chain_kernel,
            (image_shape, image_shape, image_shape),
            [padding()],
            12, where, base, start_value, defect_two, near, far, coarse,
        )

    last = chain(place, base)[2]
    before, own, _ = chain(place_later, shift(last, 16, sections))

    ends, grads = call(
        final_kernel,
        (shape(3, 256, CHANNELS, dtype=LOW), shape(SECTION, 288, CHANNELS, dtype=LOW)),
        [
            wide(), wide(), wide(),
            pltpu.VMEM((SECTION, *IMAGE), FULL),
            wide(),
            pltpu.VMEM((SECTION, *PAD_SCRATCH), LOW),
            padding(),
            pltpu.VMEM((3 * CHANNELS, CHANNELS), FULL),
        ],
        24, place, before, own, defects, leading, weights, flipped, adjoint_whole,
    )
    parts = jnp.concatenate(
        [
            ends.reshape(3, 4, 64, CHANNELS).transpose(1, 0, 2, 3).reshape(4, 192, CHANNELS),
            grads.reshape(SECTION, 4, 72, CHANNELS).transpose(1, 0, 2, 3).reshape(4, 288, CHANNELS),
        ],
        axis=1,
    )
    row_groups = [[4 * r + n for n in range(4)] for r in range(tiles // 4)]
    parts = lax.all_to_all(parts, "space", 0, 0, axis_index_groups=row_groups, tiled=True).astype(FULL)
    tile_shape = (1, 4, 2, SIDE, CHANNELS)
    section_ends = (parts[:, 0:64] + parts[:, 64:128]).reshape(tile_shape)
    start_adjoint = end_adjoint + parts[:, 128:192].reshape(tile_shape)
    weight_grad = parts[:, 192:].sum(0).reshape(SECTION, 72, CHANNELS)
    return section_ends, start_adjoint, weight_grad


def solution(mesh):
    return jax.shard_map(
        local,
        mesh=mesh,
        in_specs=(
            P(None, "space", None, None),
            P("layer", None, "space", None, None),
            P("layer", None, "space", None, None),
            P("layer", None, None),
        ),
        out_specs=(
            P("layer", None, "space", None, None),
            P("layer", None, "space", None, None),
            P("layer", "space", None),
        ),
        check_vma=False,
    )
```

```python
import jax
import jax.numpy as jnp
from jax import lax
from jax.experimental import pallas as pl
from jax.experimental.pallas import tpu as pltpu
from jax.sharding import PartitionSpec as P

STEP_SIZE = 0.1
SECTION = 4
SIDE = 32
CHANNELS = 128
PIXELS = SIDE * SIDE
PADDED = PIXELS + 2 * SIDE
PIECE = 128
CHUNK = 256
LOW = jnp.bfloat16
FULL = jnp.float32
SENT = jnp.float16

IMAGE = (PIXELS, CHANNELS)
PAD_SCRATCH = (PADDED, 3 * CHANNELS)


def clear(pad):
    edge = jnp.zeros((SIDE, 3 * CHANNELS), LOW)
    pad[0:SIDE, :] = edge
    pad[SIDE + PIXELS : PADDED, :] = edge


def put(pad, piece, values):
    column = lax.broadcasted_iota(jnp.int32, values.shape, 0) % SIDE
    left = jnp.where(column == 0, 0.0, pltpu.roll(values, 1, 0))
    right = jnp.where(column == SIDE - 1, 0.0, pltpu.roll(values, PIECE - 1, 0))
    rows = pl.ds(SIDE + piece * PIECE, PIECE)
    pad[rows, 0:CHANNELS] = left.astype(LOW)
    pad[rows, CHANNELS : 2 * CHANNELS] = values.astype(LOW)
    pad[rows, 2 * CHANNELS : 3 * CHANNELS] = right.astype(LOW)


def put_active(pad, state):
    for piece in range(PIXELS // PIECE):
        put(pad, piece, jnp.tanh(state[pl.ds(piece * PIECE, PIECE), :]))


def conv(pad, kernel, chunk):
    columns = jnp.concatenate(
        [pad[pl.ds(chunk * CHUNK + SIDE * shift, CHUNK), :] for shift in range(3)], axis=1
    )
    return jnp.dot(columns, kernel[...], preferred_element_type=FULL)


def chunks():
    return [(chunk, pl.ds(chunk * CHUNK, CHUNK)) for chunk in range(PIXELS // CHUNK)]


def relax_kernel(begin, weights, out, state, pad):
    clear(pad)
    state[...] = begin[...]

    def step(layer, carry):
        put_active(pad, state)
        for chunk, rows in chunks():
            state[rows, :] += STEP_SIZE * conv(pad, weights.at[layer], chunk)
        return carry

    lax.fori_loop(0, SECTION, step, 0)
    out[...] = state[...]


def fine_kernel(
    place, own, received, weights, closing, defect_out, send_out, closing_out, state, base, first, pad
):
    section, phase = place[0], place[1]
    clear(pad)
    closing_out[...] = closing[SECTION - 1]
    for _, rows in chunks():
        begin = jnp.where(section == 0, own[rows, :], received[rows, :])
        state[rows, :] = begin
        base[rows, :] = begin

    put_active(pad, state)
    for chunk, rows in chunks():
        term = conv(pad, weights.at[0], chunk)
        first[rows, :] = term
        state[rows, :] += STEP_SIZE * term

    @pl.when(phase == 0)
    def _():
        for chunk, rows in chunks():
            long_term = (4 * SECTION * STEP_SIZE) * conv(pad, closing.at[SECTION - 1], chunk)
            base[rows, :] += long_term

    def step(layer, carry):
        put_active(pad, state)
        for chunk, rows in chunks():
            state[rows, :] += STEP_SIZE * conv(pad, weights.at[layer], chunk)
        return carry

    lax.fori_loop(1, SECTION, step, 0)
    for _, rows in chunks():
        begin = jnp.where(section == 0, own[rows, :], received[rows, :])
        last = state[rows, :]
        defect = (last - begin) - SECTION * STEP_SIZE * first[rows, :]
        defect_out[rows, :] = defect.astype(LOW)
        send_out[0, rows, :] = jnp.where(phase == 0, last, defect)
        total = jnp.where(section == 0, begin, last - base[rows, :])
        send_out[1, rows, :] = jnp.where(phase == 0, total, defect)


def first_round_kernel(place, sent, received, leading, out, state, pad):
    phase, in_first_group = place[1], place[0] < 4

    @pl.when(phase < 2)
    def _():
        clear(pad)
        for _, rows in chunks():
            state[rows, :] = jnp.where(phase == 0, sent[0, rows, :], received[0, rows, :])
        put_active(pad, state)
        for chunk, rows in chunks():
            defect = jnp.where(phase == 0, received[0, rows, :], sent[0, rows, :])
            total = jnp.where(phase == 0, sent[1, rows, :], received[1, rows, :])
            change = SECTION * STEP_SIZE * conv(pad, leading.at[1], chunk) + defect
            out[0, rows, :] = state[rows, :] + change
            out[1, rows, :] = total + jnp.where(in_first_group, 0.0, change)

    @pl.when(phase >= 2)
    def _():
        for _, rows in chunks():
            out[0, rows, :] = jnp.where(phase == 2, sent[0, rows, :], received[0, rows, :])
            out[1, rows, :] = jnp.where(phase == 2, received[0, rows, :], sent[0, rows, :])


def closing_kernel(place, sent, received, leading, out, total, state, pad):
    phase, in_first_group = place[1], place[0] < 4
    clear(pad)
    for _, rows in chunks():
        state[rows, :] = jnp.where(phase < 2, sent[0, rows, :], received[0, rows, :])
        total[rows, :] = jnp.where(phase < 2, sent[1, rows, :], received[1, rows, :])

    def step(turn, carry):
        put_active(pad, state)
        for chunk, rows in chunks():
            defect = jnp.where(phase < 2, received[turn, rows, :], sent[turn, rows, :])
            change = SECTION * STEP_SIZE * conv(pad, leading.at[2 + turn], chunk) + defect
            state[rows, :] += change
            total[rows, :] += jnp.where(in_first_group, 0.0, change)
        return carry

    lax.fori_loop(0, 2, step, 0)
    for _, rows in chunks():
        out[rows, :] = jnp.where(in_first_group, state[rows, :], total[rows, :])


def final_kernel(place, *refs):
    stored, (ends_out, grad_out), refs = refs[:15], refs[15:17], refs[17:]
    state, begin, end, slopes, change, pads, back_pad, grads, slots = refs[:9]
    held, arrived = refs[9:16], refs[16]
    coarse, images, defects, leading, weights, flipped, end_adjoint = held
    phase, group, replica = place[1], place[2], place[3]
    targets = [slots.at[number] for number in range(8)] + list(held)
    copies = [
        pltpu.make_async_copy(source, target, arrived.at[number])
        for number, (source, target) in enumerate(zip(stored, targets))
    ]
    for copy in copies:
        copy.start()
    clear(back_pad)
    for layer in range(SECTION):
        clear(pads.at[layer])

    for copy in copies[:10]:
        copy.wait()
    for _, rows in chunks():
        state[rows, :] = slots[group, rows, :]

    def chain_step(turn, carry):
        put_active(back_pad, state)
        for chunk, rows in chunks():
            long_term = (4 * SECTION * STEP_SIZE) * conv(back_pad, coarse.at[turn], chunk)
            state[rows, :] += long_term + slots[group - turn, rows, :]
        return carry

    lax.fori_loop(1, group, chain_step, 0)
    for _, rows in chunks():
        begin[rows, :] = jnp.where(group == 0, images[rows, :], state[rows, :])

    @pl.when(group > 0)
    def _():
        chain_step(group, 0)

    for _, rows in chunks():
        end[rows, :] = state[rows, :]
        state[rows, :] = begin[rows, :]
    for copy in copies[10:]:
        copy.wait()

    def level_step(turn, carry):
        put_active(back_pad, state)
        for chunk, rows in chunks():
            state[rows, :] += (
                SECTION * STEP_SIZE * conv(back_pad, leading.at[turn], chunk)
                + defects[turn, rows, :].astype(FULL)
            )

        @pl.when(phase == turn)
        def _():
            end[...] = state[...]

        @pl.when(phase == turn + 1)
        def _():
            begin[...] = state[...]

        return carry

    lax.fori_loop(0, 3, level_step, 0)

    def active(layer):
        for piece in range(PIXELS // PIECE):
            rows = pl.ds(piece * PIECE, PIECE)
            slope = jnp.tanh(begin[rows, :])
            slopes[layer, rows, :] = STEP_SIZE * (1.0 - slope * slope)
            put(pads.at[layer], piece, slope)

    def forward(layer, carry):
        active(layer)
        for chunk, rows in chunks():
            begin[rows, :] += STEP_SIZE * conv(pads.at[layer], weights.at[layer], chunk)
        return carry

    lax.fori_loop(0, SECTION - 1, forward, 0)
    active(SECTION - 1)
    change[...] = jnp.zeros(IMAGE, FULL)

    def backward(turn, carry):
        layer = SECTION - 1 - turn
        for piece in range(PIXELS // PIECE):
            rows = pl.ds(piece * PIECE, PIECE)
            put(back_pad, piece, end_adjoint[rows, :] + change[rows, :])
        low = back_pad[pl.ds(SIDE, PIXELS), CHANNELS : 2 * CHANNELS]
        for part in range(3):
            offset = 2 * replica + part
            columns = pads[
                layer,
                pl.ds(pl.multiple_of(SIDE * (offset // 3), SIDE), PIXELS),
                pl.ds(pl.multiple_of(CHANNELS * (offset % 3), CHANNELS), CHANNELS),
            ]
            grads[pl.ds(part * CHANNELS, CHANNELS), :] = STEP_SIZE * lax.dot_general(
                columns, low, (((0,), (0,)), ((), ())), preferred_element_type=FULL
            )
        grad_out[layer] = grads[pl.ds(pl.multiple_of(SIDE * replica, SIDE), 288), :].astype(LOW)
        for chunk, rows in chunks():
            change[rows, :] += slopes[layer, rows, :] * conv(back_pad, flipped.at[layer], chunk)
        return carry

    lax.fori_loop(0, SECTION, backward, 0)
    kept = pl.ds(pl.multiple_of(replica * 256, 256), 256)
    high = end[kept, :].astype(LOW)
    ends_out[0] = high
    ends_out[1] = (end[kept, :] - high.astype(FULL)).astype(LOW)
    ends_out[2] = change[kept, :].astype(LOW)


def call(body, outs, scratch, megabytes, place, *operands, stored=()):
    held = pl.BlockSpec(memory_space=pltpu.VMEM)
    in_specs = [held] * len(operands) + [pl.BlockSpec(memory_space=pltpu.HBM)] * len(stored)
    operands += tuple(stored)
    if place is not None:
        in_specs = [pl.BlockSpec(memory_space=pltpu.SMEM)] + in_specs
        operands = (place,) + operands
    return pl.pallas_call(
        body,
        out_shape=outs,
        in_specs=in_specs,
        out_specs=jax.tree.map(lambda _: held, outs),
        scratch_shapes=scratch,
        compiler_params=pltpu.CompilerParams(vmem_limit_bytes=megabytes * 1024 * 1024),
    )(*operands)


def shape(*dims, dtype=FULL):
    return jax.ShapeDtypeStruct(dims, dtype)


def wide():
    return pltpu.VMEM(IMAGE, FULL)


def padding():
    return pltpu.VMEM(PAD_SCRATCH, LOW)


def swap(block, distance, sections):
    moved = lax.ppermute(block.astype(SENT), "layer", [(i, i ^ distance) for i in range(sections)])
    return moved.astype(block.dtype)


def shift(block, distance, sections):
    route = [(i, i + distance) for i in range(sections - distance)]
    return lax.ppermute(block.astype(SENT), "layer", route).astype(block.dtype)


def local(images, end_guess, end_adjoint, weights):
    section = lax.axis_index("layer")
    tile = lax.axis_index("space")
    sections = lax.axis_size("layer")
    tiles = lax.axis_size("space")
    replica = tile // 4
    group = section // 4
    place = jnp.stack([section, section % 4, group, replica]).astype(jnp.int32)
    rows_of_groups = [[4 * g + i for i in range(4)] for g in range(sections // 4)]
    columns_of_groups = [[4 * g + i for g in range(sections // 4)] for i in range(4)]

    guess = jnp.where(section == 0, images, shift(end_guess[0], 1, sections))
    both = jnp.stack([guess, end_adjoint[0]], axis=1).astype(SENT)
    both = lax.all_to_all(jnp.tile(both, (tiles // 4, 1, 1, 1, 1)), "space", 0, 0, tiled=True)
    both = both.astype(FULL)
    start, adjoint_whole = both[:, 0].reshape(IMAGE), both[:, 1].reshape(IMAGE)

    leading = lax.all_gather(weights[0], "layer", axis_index_groups=rows_of_groups)
    flipped = (
        weights.reshape(SECTION, 9, CHANNELS, CHANNELS)[:, ::-1]
        .transpose(0, 1, 3, 2)
        .reshape(SECTION, 9 * CHANNELS, CHANNELS)
    )
    image_shape, pair_shape = shape(*IMAGE), shape(2, *IMAGE)

    relaxed = call(relax_kernel, image_shape, [wide(), padding()], 8, None, start, weights)
    received = shift(relaxed, 1, sections)
    defect, send, closing_weights = call(
        fine_kernel,
        (shape(*IMAGE, dtype=LOW), pair_shape, shape(9 * CHANNELS, CHANNELS, dtype=LOW)),
        [wide(), wide(), wide(), padding()],
        12, place, start, received, weights, leading,
    )
    coarse = lax.all_gather(closing_weights, "layer", axis_index_groups=columns_of_groups)
    defects = lax.all_gather(defect, "layer", axis_index_groups=rows_of_groups)
    received = swap(send, 1, sections)
    send = call(first_round_kernel, pair_shape, [wide(), padding()], 10, place, send, received, leading)
    received = swap(send, 3, sections)
    defect_two, base = call(
        closing_kernel, (image_shape, image_shape), [wide(), padding()], 10, place, send, received, leading
    )
    up = [(i, (i + 4) % sections) for i in range(sections)]
    down = [(j, i) for i, j in up]
    ups, downs = [defect_two.astype(SENT)], [defect_two.astype(SENT)]
    for turn in range(4):
        ups.append(lax.ppermute(ups[-1], "layer", up))
        if turn < 3:
            downs.append(lax.ppermute(downs[-1], "layer", down))
    slots = [defect_two] + [block.astype(FULL) for block in ups[1:] + downs[:0:-1]]

    stored = (coarse, base, defects, leading, weights, flipped, adjoint_whole)
    ends, grads = call(
        final_kernel,
        (shape(3, 256, CHANNELS, dtype=LOW), shape(SECTION, 288, CHANNELS, dtype=LOW)),
        [
            wide(), wide(), wide(),
            pltpu.VMEM((SECTION, *IMAGE), FULL),
            wide(),
            pltpu.VMEM((SECTION, *PAD_SCRATCH), LOW),
            padding(),
            pltpu.VMEM((3 * CHANNELS, CHANNELS), FULL),
            pltpu.VMEM((8, *IMAGE), FULL),
            *[pltpu.VMEM(array.shape, array.dtype) for array in stored],
            pltpu.SemaphoreType.DMA((8 + len(stored),)),
        ],
        60, place, stored=(*slots, *stored),
    )
    parts = jnp.concatenate(
        [
            ends.reshape(3, 4, 64, CHANNELS).transpose(1, 0, 2, 3).reshape(4, 192, CHANNELS),
            grads.reshape(SECTION, 4, 72, CHANNELS).transpose(1, 0, 2, 3).reshape(4, 288, CHANNELS),
        ],
        axis=1,
    )
    row_groups = [[4 * r + n for n in range(4)] for r in range(tiles // 4)]
    parts = lax.all_to_all(parts, "space", 0, 0, axis_index_groups=row_groups, tiled=True).astype(FULL)
    tile_shape = (1, 4, 2, SIDE, CHANNELS)
    section_ends = (parts[:, 0:64] + parts[:, 64:128]).reshape(tile_shape)
    start_adjoint = end_adjoint + parts[:, 128:192].reshape(tile_shape)
    weight_grad = parts[:, 192:].sum(0).reshape(SECTION, 72, CHANNELS)
    return section_ends, start_adjoint, weight_grad


def solution(mesh):
    return jax.shard_map(
        local,
        mesh=mesh,
        in_specs=(
            P(None, "space", None, None),
            P("layer", None, "space", None, None),
            P("layer", None, "space", None, None),
            P("layer", None, None),
        ),
        out_specs=(
            P("layer", None, "space", None, None),
            P("layer", None, "space", None, None),
            P("layer", "space", None),
        ),
        check_vma=False,
    )
```

```python
import jax
import jax.numpy as jnp
from jax import lax
from jax.experimental import pallas as pl
from jax.experimental.pallas import tpu as pltpu
from jax.sharding import PartitionSpec as P

STEP_SIZE = 0.1
SECTION = 4
SIDE = 32
CHANNELS = 128
PIXELS = SIDE * SIDE
PADDED = PIXELS + 2 * SIDE
PIECE = 128
CHUNK = 256
LOW = jnp.bfloat16
FULL = jnp.float32
SENT = jnp.float16

IMAGE = (PIXELS, CHANNELS)
PAD_SCRATCH = (PADDED, 3 * CHANNELS)


def clear(pad):
    edge = jnp.zeros((SIDE, 3 * CHANNELS), LOW)
    pad[0:SIDE, :] = edge
    pad[SIDE + PIXELS : PADDED, :] = edge


def put(pad, piece, values):
    column = lax.broadcasted_iota(jnp.int32, values.shape, 0) % SIDE
    left = jnp.where(column == 0, 0.0, pltpu.roll(values, 1, 0))
    right = jnp.where(column == SIDE - 1, 0.0, pltpu.roll(values, PIECE - 1, 0))
    rows = pl.ds(SIDE + piece * PIECE, PIECE)
    pad[rows, 0:CHANNELS] = left.astype(LOW)
    pad[rows, CHANNELS : 2 * CHANNELS] = values.astype(LOW)
    pad[rows, 2 * CHANNELS : 3 * CHANNELS] = right.astype(LOW)


def put_active(pad, state):
    for piece in range(PIXELS // PIECE):
        put(pad, piece, jnp.tanh(state[pl.ds(piece * PIECE, PIECE), :]))


def conv(pad, kernel, chunk):
    columns = jnp.concatenate(
        [pad[pl.ds(chunk * CHUNK + SIDE * shift, CHUNK), :] for shift in range(3)], axis=1
    )
    return jnp.dot(columns, kernel[...], preferred_element_type=FULL)


def chunks():
    return [(chunk, pl.ds(chunk * CHUNK, CHUNK)) for chunk in range(PIXELS // CHUNK)]


def relax_kernel(begin, weights, out, state, pad):
    clear(pad)
    state[...] = begin[...]

    def step(layer, carry):
        put_active(pad, state)
        for chunk, rows in chunks():
            state[rows, :] += STEP_SIZE * conv(pad, weights.at[layer], chunk)
        return carry

    lax.fori_loop(0, SECTION, step, 0)
    out[...] = state[...]


def fine_kernel(place, own, received, weights, closing, defect_out, send_out, state, base, first, pad):
    section, phase = place[0], place[1]
    clear(pad)
    for _, rows in chunks():
        begin = jnp.where(section == 0, own[rows, :], received[rows, :])
        state[rows, :] = begin
        base[rows, :] = begin

    put_active(pad, state)
    for chunk, rows in chunks():
        term = conv(pad, weights.at[0], chunk)
        first[rows, :] = term
        state[rows, :] += STEP_SIZE * term

    @pl.when(phase == 0)
    def _():
        for chunk, rows in chunks():
            long_term = (4 * SECTION * STEP_SIZE) * conv(pad, closing.at[SECTION - 1], chunk)
            base[rows, :] += long_term

    def step(layer, carry):
        put_active(pad, state)
        for chunk, rows in chunks():
            state[rows, :] += STEP_SIZE * conv(pad, weights.at[layer], chunk)
        return carry

    lax.fori_loop(1, SECTION, step, 0)
    for _, rows in chunks():
        begin = jnp.where(section == 0, own[rows, :], received[rows, :])
        last = state[rows, :]
        defect = (last - begin) - SECTION * STEP_SIZE * first[rows, :]
        defect_out[rows, :] = defect.astype(LOW)
        send_out[0, rows, :] = jnp.where(phase == 0, last, defect)
        total = jnp.where(section == 0, begin, last - base[rows, :])
        send_out[1, rows, :] = jnp.where(phase == 0, total, defect)


def first_round_kernel(place, sent, received, leading, out, state, pad):
    phase, in_first_group = place[1], place[0] < 4

    @pl.when(phase < 2)
    def _():
        clear(pad)
        for _, rows in chunks():
            state[rows, :] = jnp.where(phase == 0, sent[0, rows, :], received[0, rows, :])
        put_active(pad, state)
        for chunk, rows in chunks():
            defect = jnp.where(phase == 0, received[0, rows, :], sent[0, rows, :])
            total = jnp.where(phase == 0, sent[1, rows, :], received[1, rows, :])
            change = SECTION * STEP_SIZE * conv(pad, leading.at[1], chunk) + defect
            out[0, rows, :] = state[rows, :] + change
            out[1, rows, :] = total + jnp.where(in_first_group, 0.0, change)

    @pl.when(phase >= 2)
    def _():
        for _, rows in chunks():
            out[0, rows, :] = jnp.where(phase == 2, sent[0, rows, :], received[0, rows, :])
            out[1, rows, :] = jnp.where(phase == 2, received[0, rows, :], sent[0, rows, :])


def closing_kernel(place, sent, received, leading, out, total, state, pad):
    phase, in_first_group = place[1], place[0] < 4
    clear(pad)
    for _, rows in chunks():
        state[rows, :] = jnp.where(phase < 2, sent[0, rows, :], received[0, rows, :])
        total[rows, :] = jnp.where(phase < 2, sent[1, rows, :], received[1, rows, :])

    def step(turn, carry):
        put_active(pad, state)
        for chunk, rows in chunks():
            defect = jnp.where(phase < 2, received[turn, rows, :], sent[turn, rows, :])
            change = SECTION * STEP_SIZE * conv(pad, leading.at[2 + turn], chunk) + defect
            state[rows, :] += change
            total[rows, :] += jnp.where(in_first_group, 0.0, change)
        return carry

    lax.fori_loop(0, 2, step, 0)
    for _, rows in chunks():
        out[rows, :] = jnp.where(in_first_group, state[rows, :], total[rows, :])


def load(sources, targets, arrived):
    copies = [
        pltpu.make_async_copy(source, target, arrived.at[number])
        for number, (source, target) in enumerate(zip(sources, targets))
    ]
    for copy in copies:
        copy.start()
    return copies


def chain_kernel(place, *refs):
    stored, outs, (state, begin, pad, slots, coarse, images, arrived) = refs[:10], refs[10:12], refs[12:]
    group = place[2]
    copies = load(stored, [slots.at[number] for number in range(8)] + [coarse, images], arrived)
    clear(pad)
    for copy in copies:
        copy.wait()
    for _, rows in chunks():
        state[rows, :] = slots[group, rows, :]

    def chain_step(turn, carry):
        put_active(pad, state)
        for chunk, rows in chunks():
            long_term = (4 * SECTION * STEP_SIZE) * conv(pad, coarse.at[turn], chunk)
            state[rows, :] += long_term + slots[group - turn, rows, :]
        return carry

    lax.fori_loop(1, group, chain_step, 0)
    for _, rows in chunks():
        begin[rows, :] = jnp.where(group == 0, images[rows, :], state[rows, :])

    @pl.when(group > 0)
    def _():
        chain_step(group, 0)

    for copy in load([begin, state], outs, arrived):
        copy.wait()


def final_kernel(place, *refs):
    stored, (ends_out, grad_out), refs = refs[:7], refs[7:9], refs[9:]
    begin, slopes, change, pads, back_pad, grads = refs[:6]
    held, arrived = refs[6:13], refs[13]
    state, end, defects, leading, weights, flipped, end_adjoint = held
    phase, replica = place[1], place[3]
    copies = load(stored, held, arrived)
    clear(back_pad)
    for layer in range(SECTION):
        clear(pads.at[layer])
    for copy in copies[:4]:
        copy.wait()
    begin[...] = state[...]

    def level_step(turn, carry):
        put_active(back_pad, state)
        for chunk, rows in chunks():
            state[rows, :] += (
                SECTION * STEP_SIZE * conv(back_pad, leading.at[turn], chunk)
                + defects[turn, rows, :].astype(FULL)
            )

        @pl.when(phase == turn)
        def _():
            end[...] = state[...]

        @pl.when(phase == turn + 1)
        def _():
            begin[...] = state[...]

        return carry

    lax.fori_loop(0, 3, level_step, 0)
    for copy in copies[4:]:
        copy.wait()

    def active(layer):
        for piece in range(PIXELS // PIECE):
            rows = pl.ds(piece * PIECE, PIECE)
            slope = jnp.tanh(begin[rows, :])
            slopes[layer, rows, :] = STEP_SIZE * (1.0 - slope * slope)
            put(pads.at[layer], piece, slope)

    def forward(layer, carry):
        active(layer)
        for chunk, rows in chunks():
            begin[rows, :] += STEP_SIZE * conv(pads.at[layer], weights.at[layer], chunk)
        return carry

    lax.fori_loop(0, SECTION - 1, forward, 0)
    active(SECTION - 1)
    change[...] = jnp.zeros(IMAGE, FULL)

    def backward(turn, carry):
        layer = SECTION - 1 - turn
        for piece in range(PIXELS // PIECE):
            rows = pl.ds(piece * PIECE, PIECE)
            put(back_pad, piece, end_adjoint[rows, :] + change[rows, :])
        low = back_pad[pl.ds(SIDE, PIXELS), CHANNELS : 2 * CHANNELS]
        for part in range(3):
            offset = 2 * replica + part
            columns = pads[
                layer,
                pl.ds(pl.multiple_of(SIDE * (offset // 3), SIDE), PIXELS),
                pl.ds(pl.multiple_of(CHANNELS * (offset % 3), CHANNELS), CHANNELS),
            ]
            grads[pl.ds(part * CHANNELS, CHANNELS), :] = STEP_SIZE * lax.dot_general(
                columns, low, (((0,), (0,)), ((), ())), preferred_element_type=FULL
            )
        grad_out[layer] = grads[pl.ds(pl.multiple_of(SIDE * replica, SIDE), 288), :].astype(LOW)
        for chunk, rows in chunks():
            change[rows, :] += slopes[layer, rows, :] * conv(back_pad, flipped.at[layer], chunk)
        return carry

    lax.fori_loop(0, SECTION, backward, 0)
    kept = pl.ds(pl.multiple_of(replica * 256, 256), 256)
    high = end[kept, :].astype(LOW)
    ends_out[0] = high
    ends_out[1] = (end[kept, :] - high.astype(FULL)).astype(LOW)
    ends_out[2] = change[kept, :].astype(LOW)


def call(body, outs, scratch, megabytes, place, *operands, stored=(), store=False):
    held = pl.BlockSpec(memory_space=pltpu.VMEM)
    in_specs = [held] * len(operands) + [pl.BlockSpec(memory_space=pltpu.HBM)] * len(stored)
    operands += tuple(stored)
    if place is not None:
        in_specs = [pl.BlockSpec(memory_space=pltpu.SMEM)] + in_specs
        operands = (place,) + operands
    return pl.pallas_call(
        body,
        out_shape=outs,
        in_specs=in_specs,
        out_specs=jax.tree.map(lambda _: pl.BlockSpec(memory_space=pltpu.HBM) if store else held, outs),
        scratch_shapes=scratch,
        compiler_params=pltpu.CompilerParams(vmem_limit_bytes=megabytes * 1024 * 1024),
    )(*operands)


def shape(*dims, dtype=FULL):
    return jax.ShapeDtypeStruct(dims, dtype)


def wide():
    return pltpu.VMEM(IMAGE, FULL)


def padding():
    return pltpu.VMEM(PAD_SCRATCH, LOW)


def swap(block, distance, sections):
    moved = lax.ppermute(block.astype(SENT), "layer", [(i, i ^ distance) for i in range(sections)])
    return moved.astype(block.dtype)


def shift(block, distance, sections):
    route = [(i, i + distance) for i in range(sections - distance)]
    return lax.ppermute(block.astype(SENT), "layer", route).astype(block.dtype)


def local(images, end_guess, end_adjoint, weights):
    section = lax.axis_index("layer")
    tile = lax.axis_index("space")
    sections = lax.axis_size("layer")
    tiles = lax.axis_size("space")
    replica = tile // 4
    group = section // 4
    place = jnp.stack([section, section % 4, group, replica]).astype(jnp.int32)
    rows_of_groups = [[4 * g + i for i in range(4)] for g in range(sections // 4)]
    columns_of_groups = [[4 * g + i for g in range(sections // 4)] for i in range(4)]

    guess, leading = lax.optimization_barrier((end_guess[0].astype(SENT), weights[0]))
    leading = lax.all_gather(leading, "layer", axis_index_groups=rows_of_groups)
    guess = jnp.where(section == 0, images, shift(guess, 1, sections).astype(FULL))
    both = jnp.stack([guess, end_adjoint[0]], axis=1).astype(SENT)
    both = lax.all_to_all(jnp.tile(both, (tiles // 4, 1, 1, 1, 1)), "space", 0, 0, tiled=True)
    both = both.astype(FULL)
    start, adjoint_whole = both[:, 0].reshape(IMAGE), both[:, 1].reshape(IMAGE)

    flipped = (
        weights.reshape(SECTION, 9, CHANNELS, CHANNELS)[:, ::-1]
        .transpose(0, 1, 3, 2)
        .reshape(SECTION, 9 * CHANNELS, CHANNELS)
    )
    image_shape, pair_shape = shape(*IMAGE), shape(2, *IMAGE)

    relaxed = call(relax_kernel, image_shape, [wide(), padding()], 8, None, start, weights)
    closing_weights, _ = lax.optimization_barrier((leading[3], relaxed))
    received = shift(relaxed, 1, sections)
    coarse = lax.all_gather(closing_weights, "layer", axis_index_groups=columns_of_groups)
    defect, send = call(
        fine_kernel,
        (shape(*IMAGE, dtype=LOW), pair_shape),
        [wide(), wide(), wide(), padding()],
        12, place, start, received, weights, leading,
    )
    defects = lax.all_gather(defect, "layer", axis_index_groups=rows_of_groups)
    received = swap(send, 1, sections)
    send = call(first_round_kernel, pair_shape, [wide(), padding()], 10, place, send, received, leading)
    received = swap(send, 3, sections)
    defect_two, base = call(
        closing_kernel, (image_shape, image_shape), [wide(), padding()], 10, place, send, received, leading
    )
    up = [(i, (i + 4) % sections) for i in range(sections)]
    down = [(j, i) for i, j in up]
    ups, downs, widened = [defect_two.astype(SENT)], [defect_two.astype(SENT)], {}
    for turn in range(4):
        moved = [lax.ppermute(ups[-1], "layer", up)]
        if turn < 3:
            moved.append(lax.ppermute(downs[-1], "layer", down))
        if turn:
            ready = [ups[-1].astype(FULL), downs[-1].astype(FULL)]
            moved, (widened[turn], widened[8 - turn]) = lax.optimization_barrier((moved, ready))
        ups.append(moved[0])
        if turn < 3:
            downs.append(moved[1])
    widened[4] = ups[-1].astype(FULL)
    slots = [defect_two] + [widened[distance] for distance in range(1, 8)]

    def scratch_like(*arrays):
        return [pltpu.VMEM(array.shape, array.dtype) for array in arrays]

    before, own = call(
        chain_kernel,
        (image_shape, image_shape),
        [
            wide(), wide(), padding(),
            pltpu.VMEM((8, *IMAGE), FULL),
            *scratch_like(coarse, base),
            pltpu.SemaphoreType.DMA((10,)),
        ],
        60, place, stored=(*slots, coarse, base), store=True,
    )
    stored = (before, own, defects, leading, weights, flipped, adjoint_whole)
    ends, grads = call(
        final_kernel,
        (shape(3, 256, CHANNELS, dtype=LOW), shape(SECTION, 288, CHANNELS, dtype=LOW)),
        [
            wide(),
            pltpu.VMEM((SECTION, *IMAGE), FULL),
            wide(),
            pltpu.VMEM((SECTION, *PAD_SCRATCH), LOW),
            padding(),
            pltpu.VMEM((3 * CHANNELS, CHANNELS), FULL),
            *scratch_like(*stored),
            pltpu.SemaphoreType.DMA((len(stored),)),
        ],
        60, place, stored=stored,
    )
    parts = jnp.concatenate(
        [
            ends.reshape(3, 4, 64, CHANNELS).transpose(1, 0, 2, 3).reshape(4, 192, CHANNELS),
            grads.reshape(SECTION, 4, 72, CHANNELS).transpose(1, 0, 2, 3).reshape(4, 288, CHANNELS),
        ],
        axis=1,
    )
    row_groups = [[4 * r + n for n in range(4)] for r in range(tiles // 4)]
    parts = lax.all_to_all(parts, "space", 0, 0, axis_index_groups=row_groups, tiled=True).astype(FULL)
    tile_shape = (1, 4, 2, SIDE, CHANNELS)
    section_ends = (parts[:, 0:64] + parts[:, 64:128]).reshape(tile_shape)
    start_adjoint = end_adjoint + parts[:, 128:192].reshape(tile_shape)
    weight_grad = parts[:, 192:].sum(0).reshape(SECTION, 72, CHANNELS)
    return section_ends, start_adjoint, weight_grad


def solution(mesh):
    return jax.shard_map(
        local,
        mesh=mesh,
        in_specs=(
            P(None, "space", None, None),
            P("layer", None, "space", None, None),
            P("layer", None, "space", None, None),
            P("layer", None, None),
        ),
        out_specs=(
            P("layer", None, "space", None, None),
            P("layer", None, "space", None, None),
            P("layer", "space", None),
        ),
        check_vma=False,
    )
```

```python
import jax
import jax.numpy as jnp
from jax import lax
from jax.experimental import pallas as pl
from jax.experimental.pallas import tpu as pltpu
from jax.sharding import PartitionSpec as P

STEP_SIZE = 0.1
SECTION = 4
SIDE = 32
CHANNELS = 128
PIXELS = SIDE * SIDE
PADDED = PIXELS + 2 * SIDE
PIECE = 128
CHUNK = 256
LOW = jnp.bfloat16
FULL = jnp.float32
SENT = jnp.float16

IMAGE = (PIXELS, CHANNELS)
PAD_SCRATCH = (PADDED, 3 * CHANNELS)


def clear(pad):
    edge = jnp.zeros((SIDE, 3 * CHANNELS), LOW)
    pad[0:SIDE, :] = edge
    pad[SIDE + PIXELS : PADDED, :] = edge


def put(pad, piece, values):
    column = lax.broadcasted_iota(jnp.int32, values.shape, 0) % SIDE
    left = jnp.where(column == 0, 0.0, pltpu.roll(values, 1, 0))
    right = jnp.where(column == SIDE - 1, 0.0, pltpu.roll(values, PIECE - 1, 0))
    rows = pl.ds(SIDE + piece * PIECE, PIECE)
    pad[rows, 0:CHANNELS] = left.astype(LOW)
    pad[rows, CHANNELS : 2 * CHANNELS] = values.astype(LOW)
    pad[rows, 2 * CHANNELS : 3 * CHANNELS] = right.astype(LOW)


def put_active(pad, state):
    for piece in range(PIXELS // PIECE):
        put(pad, piece, jnp.tanh(state[pl.ds(piece * PIECE, PIECE), :]))


def conv(pad, kernel, chunk):
    columns = jnp.concatenate(
        [pad[pl.ds(chunk * CHUNK + SIDE * shift, CHUNK), :] for shift in range(3)], axis=1
    )
    return jnp.dot(columns, kernel[...], preferred_element_type=FULL)


def chunks():
    return [(chunk, pl.ds(chunk * CHUNK, CHUNK)) for chunk in range(PIXELS // CHUNK)]


def load(sources, targets, arrived):
    copies = [
        pltpu.make_async_copy(source, target, arrived.at[number])
        for number, (source, target) in enumerate(zip(sources, targets))
    ]
    for copy in copies:
        copy.start()
    return copies


def fine_kernel(
    place, start, previous_stored, weights_stored, leading_stored,
    send_out, defect_out, closing_out,
    state, begin, base, first, pad, previous, weights, closing, defect, arrived,
):
    section, phase = place[0], place[1]
    last_leading = leading_stored.at[SECTION - 1]
    copies = load(
        [previous_stored, weights_stored, last_leading, last_leading],
        [previous, weights, closing, closing_out],
        arrived,
    )
    clear(pad)
    state[...] = start[...]
    copies[0].wait()

    def relax(layer, carry):
        put_active(pad, state)
        for chunk, rows in chunks():
            state[rows, :] += STEP_SIZE * conv(pad, previous.at[layer], chunk)
        return carry

    lax.fori_loop(0, SECTION, relax, 0)
    for _, rows in chunks():
        value = jnp.where(section == 0, start[rows, :], state[rows, :])
        state[rows, :] = value
        begin[rows, :] = value
        base[rows, :] = value
    copies[1].wait()
    copies[2].wait()

    put_active(pad, state)
    for chunk, rows in chunks():
        term = conv(pad, weights.at[0], chunk)
        first[rows, :] = term
        state[rows, :] += STEP_SIZE * term

    @pl.when(phase == 0)
    def _():
        for chunk, rows in chunks():
            base[rows, :] += (4 * SECTION * STEP_SIZE) * conv(pad, closing, chunk)

    def step(layer, carry):
        put_active(pad, state)
        for chunk, rows in chunks():
            state[rows, :] += STEP_SIZE * conv(pad, weights.at[layer], chunk)
        return carry

    lax.fori_loop(1, SECTION, step, 0)
    for _, rows in chunks():
        last = state[rows, :]
        term = (last - begin[rows, :]) - SECTION * STEP_SIZE * first[rows, :]
        defect[rows, :] = term.astype(LOW)
        send_out[0, rows, :] = jnp.where(phase == 0, last, term)
        total = jnp.where(section == 0, begin[rows, :], last - base[rows, :])
        send_out[1, rows, :] = jnp.where(phase == 0, total, term)
    copies[3].wait()
    for copy in load([defect], [defect_out], arrived):
        copy.wait()


def first_round_kernel(place, sent, received, leading, out, state, pad):
    phase, in_first_group = place[1], place[0] < 4

    @pl.when(phase < 2)
    def _():
        clear(pad)
        for _, rows in chunks():
            state[rows, :] = jnp.where(phase == 0, sent[0, rows, :], received[0, rows, :])
        put_active(pad, state)
        for chunk, rows in chunks():
            defect = jnp.where(phase == 0, received[0, rows, :], sent[0, rows, :])
            total = jnp.where(phase == 0, sent[1, rows, :], received[1, rows, :])
            change = SECTION * STEP_SIZE * conv(pad, leading.at[1], chunk) + defect
            out[0, rows, :] = state[rows, :] + change
            out[1, rows, :] = total + jnp.where(in_first_group, 0.0, change)

    @pl.when(phase >= 2)
    def _():
        for _, rows in chunks():
            out[0, rows, :] = jnp.where(phase == 2, sent[0, rows, :], received[0, rows, :])
            out[1, rows, :] = jnp.where(phase == 2, received[0, rows, :], sent[0, rows, :])


def closing_kernel(place, sent, received, leading, out, total, state, pad):
    phase, in_first_group = place[1], place[0] < 4
    clear(pad)
    for _, rows in chunks():
        state[rows, :] = jnp.where(phase < 2, sent[0, rows, :], received[0, rows, :])
        total[rows, :] = jnp.where(phase < 2, sent[1, rows, :], received[1, rows, :])

    def step(turn, carry):
        put_active(pad, state)
        for chunk, rows in chunks():
            defect = jnp.where(phase < 2, received[turn, rows, :], sent[turn, rows, :])
            change = SECTION * STEP_SIZE * conv(pad, leading.at[2 + turn], chunk) + defect
            state[rows, :] += change
            total[rows, :] += jnp.where(in_first_group, 0.0, change)
        return carry

    lax.fori_loop(0, 2, step, 0)
    for _, rows in chunks():
        out[rows, :] = jnp.where(in_first_group, state[rows, :], total[rows, :])


def chain_kernel(place, *refs):
    stored, outs, (state, begin, pad, slots, coarse, images, arrived) = refs[:10], refs[10:12], refs[12:]
    group = place[2]
    copies = load(stored, [slots.at[number] for number in range(8)] + [coarse, images], arrived)
    clear(pad)
    for copy in copies:
        copy.wait()
    for _, rows in chunks():
        state[rows, :] = slots[group, rows, :]

    def chain_step(turn, carry):
        put_active(pad, state)
        for chunk, rows in chunks():
            long_term = (4 * SECTION * STEP_SIZE) * conv(pad, coarse.at[turn], chunk)
            state[rows, :] += long_term + slots[group - turn, rows, :]
        return carry

    lax.fori_loop(1, group, chain_step, 0)
    for _, rows in chunks():
        begin[rows, :] = jnp.where(group == 0, images[rows, :], state[rows, :])

    @pl.when(group > 0)
    def _():
        chain_step(group, 0)

    for copy in load([begin, state], outs, arrived):
        copy.wait()


def final_kernel(place, *refs):
    stored, out, refs = refs[:7], refs[7], refs[8:]
    begin, slopes, change, pads, back_pad, grads = refs[:6]
    held, arrived = refs[6:13], refs[13]
    state, end, defects, leading, weights, flipped, end_adjoint = held
    phase, replica = place[1], place[3]
    copies = load(stored, held, arrived)
    clear(back_pad)
    for layer in range(SECTION):
        clear(pads.at[layer])
    for copy in copies[:4]:
        copy.wait()
    begin[...] = state[...]
    grads[3 * CHANNELS :, :] = jnp.zeros((8, CHANNELS), FULL)

    def level_step(turn, carry):
        put_active(back_pad, state)
        for chunk, rows in chunks():
            state[rows, :] += (
                SECTION * STEP_SIZE * conv(back_pad, leading.at[turn], chunk)
                + defects[turn, rows, :].astype(FULL)
            )

        @pl.when(phase == turn)
        def _():
            end[...] = state[...]

        @pl.when(phase == turn + 1)
        def _():
            begin[...] = state[...]

        return carry

    lax.fori_loop(0, 3, level_step, 0)
    for copy in copies[4:]:
        copy.wait()

    def active(layer):
        for piece in range(PIXELS // PIECE):
            rows = pl.ds(piece * PIECE, PIECE)
            slope = jnp.tanh(begin[rows, :])
            slopes[layer, rows, :] = STEP_SIZE * (1.0 - slope * slope)
            put(pads.at[layer], piece, slope)

    def forward(layer, carry):
        active(layer)
        for chunk, rows in chunks():
            begin[rows, :] += STEP_SIZE * conv(pads.at[layer], weights.at[layer], chunk)
        return carry

    lax.fori_loop(0, SECTION - 1, forward, 0)
    active(SECTION - 1)
    change[...] = jnp.zeros(IMAGE, FULL)

    def backward(turn, carry):
        layer = SECTION - 1 - turn
        for piece in range(PIXELS // PIECE):
            rows = pl.ds(piece * PIECE, PIECE)
            put(back_pad, piece, end_adjoint[rows, :] + change[rows, :])
        low = back_pad[pl.ds(SIDE, PIXELS), CHANNELS : 2 * CHANNELS]
        for part in range(3):
            offset = 2 * replica + part
            columns = pads[
                layer,
                pl.ds(pl.multiple_of(SIDE * (offset // 3), SIDE), PIXELS),
                pl.ds(pl.multiple_of(CHANNELS * (offset % 3), CHANNELS), CHANNELS),
            ]
            grads[pl.ds(part * CHANNELS, CHANNELS), :] = STEP_SIZE * lax.dot_general(
                columns, low, (((0,), (0,)), ((), ())), preferred_element_type=FULL
            )
        for block in range(4):
            rows = pl.ds(pl.multiple_of(SIDE * replica + 72 * block, 8), 80)
            out[block, pl.ds(pl.multiple_of(192 + 80 * layer, 16), 80), :] = grads[rows, :].astype(LOW)
        for chunk, rows in chunks():
            change[rows, :] += slopes[layer, rows, :] * conv(back_pad, flipped.at[layer], chunk)
        return carry

    lax.fori_loop(0, SECTION, backward, 0)
    for block in range(4):
        kept = pl.ds(pl.multiple_of(replica * 256 + block * 64, 64), 64)
        high = end[kept, :].astype(LOW)
        out[block, 0:64, :] = high
        out[block, 64:128, :] = (end[kept, :] - high.astype(FULL)).astype(LOW)
        out[block, 128:192, :] = change[kept, :].astype(LOW)


def call(body, outs, scratch, megabytes, place, *operands, stored=(), store=()):
    held = pl.BlockSpec(memory_space=pltpu.VMEM)
    in_specs = [held] * len(operands) + [pl.BlockSpec(memory_space=pltpu.HBM)] * len(stored)
    operands += tuple(stored)
    if place is not None:
        in_specs = [pl.BlockSpec(memory_space=pltpu.SMEM)] + in_specs
        operands = (place,) + operands
    return pl.pallas_call(
        body,
        out_shape=outs,
        in_specs=in_specs,
        out_specs=jax.tree.unflatten(
            jax.tree.structure(outs),
            [pl.BlockSpec(memory_space=pltpu.HBM) if n in store else held for n in range(len(jax.tree.leaves(outs)))],
        ),
        scratch_shapes=scratch,
        compiler_params=pltpu.CompilerParams(vmem_limit_bytes=megabytes * 1024 * 1024),
    )(*operands)


def shape(*dims, dtype=FULL):
    return jax.ShapeDtypeStruct(dims, dtype)


def wide():
    return pltpu.VMEM(IMAGE, FULL)


def padding():
    return pltpu.VMEM(PAD_SCRATCH, LOW)


def swap(block, distance, sections):
    moved = lax.ppermute(block.astype(SENT), "layer", [(i, i ^ distance) for i in range(sections)])
    return moved.astype(block.dtype)


def shift(block, distance, sections):
    route = [(i, i + distance) for i in range(sections - distance)]
    return lax.ppermute(block.astype(SENT), "layer", route).astype(block.dtype)


def local(images, end_guess, end_adjoint, weights):
    section = lax.axis_index("layer")
    tile = lax.axis_index("space")
    sections = lax.axis_size("layer")
    tiles = lax.axis_size("space")
    replica = tile // 4
    group = section // 4
    place = jnp.stack([section, section % 4, group, replica]).astype(jnp.int32)
    rows_of_groups = [[4 * g + i for i in range(4)] for g in range(sections // 4)]
    columns_of_groups = [[4 * g + i for g in range(sections // 4)] for i in range(4)]

    guess, leading = lax.optimization_barrier((end_guess[0].astype(SENT), weights[0]))
    leading = lax.all_gather(leading, "layer", axis_index_groups=rows_of_groups)
    previous = lax.ppermute(weights, "layer", [(i, i + 1) for i in range(sections - 1)])
    guess = jnp.where(section < 2, images, shift(guess, 2, sections).astype(FULL))
    both = jnp.stack([guess, end_adjoint[0]], axis=1).astype(SENT)
    both = lax.all_to_all(jnp.tile(both, (tiles // 4, 1, 1, 1, 1)), "space", 0, 0, tiled=True)
    both = both.astype(FULL)
    start, adjoint_whole = both[:, 0].reshape(IMAGE), both[:, 1].reshape(IMAGE)

    flipped = (
        weights.reshape(SECTION, 9, CHANNELS, CHANNELS)[:, ::-1]
        .transpose(0, 1, 3, 2)
        .reshape(SECTION, 9 * CHANNELS, CHANNELS)
    )
    image_shape, pair_shape = shape(*IMAGE), shape(2, *IMAGE)

    def scratch_like(*arrays):
        return [pltpu.VMEM(array.shape, array.dtype) for array in arrays]

    low_shape = shape(*IMAGE, dtype=LOW)
    send, defect, closing_weights = call(
        fine_kernel,
        (pair_shape, low_shape, shape(9 * CHANNELS, CHANNELS, dtype=LOW)),
        [
            wide(), wide(), wide(), wide(), padding(),
            *scratch_like(weights, weights, weights[0], low_shape),
            pltpu.SemaphoreType.DMA((4,)),
        ],
        60, place, start, stored=(previous, weights, leading), store=(1, 2),
    )
    coarse = lax.all_gather(closing_weights, "layer", axis_index_groups=columns_of_groups)
    defects = lax.all_gather(defect, "layer", axis_index_groups=rows_of_groups)
    received = swap(send, 1, sections)
    send = call(first_round_kernel, pair_shape, [wide(), padding()], 10, place, send, received, leading)
    received = swap(send, 3, sections)
    defect_two, base = call(
        closing_kernel, (image_shape, image_shape), [wide(), padding()], 10, place, send, received, leading
    )
    up = [(i, (i + 4) % sections) for i in range(sections)]
    down = [(j, i) for i, j in up]
    ups, downs, widened = [defect_two.astype(SENT)], [defect_two.astype(SENT)], {}
    for turn in range(4):
        moved = [lax.ppermute(ups[-1], "layer", up)]
        if turn < 3:
            moved.append(lax.ppermute(downs[-1], "layer", down))
        if turn:
            ready = [ups[-1].astype(FULL), downs[-1].astype(FULL)]
            moved, (widened[turn], widened[8 - turn]) = lax.optimization_barrier((moved, ready))
        ups.append(moved[0])
        if turn < 3:
            downs.append(moved[1])
    widened[4] = ups[-1].astype(FULL)
    slots = [defect_two] + [widened[distance] for distance in range(1, 8)]

    before, own = call(
        chain_kernel,
        (image_shape, image_shape),
        [
            wide(), wide(), padding(),
            pltpu.VMEM((8, *IMAGE), FULL),
            *scratch_like(coarse, base),
            pltpu.SemaphoreType.DMA((10,)),
        ],
        60, place, stored=(*slots, coarse, base), store=(0, 1),
    )
    stored = (before, own, defects, leading, weights, flipped, adjoint_whole)
    parts = call(
        final_kernel,
        shape(4, 512, CHANNELS, dtype=LOW),
        [
            wide(),
            pltpu.VMEM((SECTION, *IMAGE), FULL),
            wide(),
            pltpu.VMEM((SECTION, *PAD_SCRATCH), LOW),
            padding(),
            pltpu.VMEM((3 * CHANNELS + 8, CHANNELS), FULL),
            *scratch_like(*stored),
            pltpu.SemaphoreType.DMA((len(stored),)),
        ],
        60, place, stored=stored,
    )
    row_groups = [[4 * r + n for n in range(4)] for r in range(tiles // 4)]
    parts = lax.all_to_all(parts, "space", 0, 0, axis_index_groups=row_groups, tiled=True).astype(FULL)
    tile_shape = (1, 4, 2, SIDE, CHANNELS)
    section_ends = (parts[:, 0:64] + parts[:, 64:128]).reshape(tile_shape)
    start_adjoint = end_adjoint + parts[:, 128:192].reshape(tile_shape)
    weight_grad = parts[:, 192:].sum(0).reshape(SECTION, 80, CHANNELS)[:, :72]
    return section_ends, start_adjoint, weight_grad


def solution(mesh):
    return jax.shard_map(
        local,
        mesh=mesh,
        in_specs=(
            P(None, "space", None, None),
            P("layer", None, "space", None, None),
            P("layer", None, "space", None, None),
            P("layer", None, None),
        ),
        out_specs=(
            P("layer", None, "space", None, None),
            P("layer", None, "space", None, None),
            P("layer", "space", None),
        ),
        check_vma=False,
    )
```

```python
import jax
import jax.numpy as jnp
from jax import lax
from jax.experimental import pallas as pl
from jax.experimental.pallas import tpu as pltpu
from jax.sharding import PartitionSpec as P

STEP_SIZE = 0.1
SECTION = 4
SIDE = 32
CHANNELS = 128
PIXELS = SIDE * SIDE
PADDED = PIXELS + 2 * SIDE
PIECE = 128
CHUNK = 256
LOW = jnp.bfloat16
FULL = jnp.float32
SENT = jnp.float16

IMAGE = (PIXELS, CHANNELS)
PAD_SCRATCH = (PADDED, 3 * CHANNELS)


def clear(pad):
    edge = jnp.zeros((SIDE, 3 * CHANNELS), LOW)
    pad[0:SIDE, :] = edge
    pad[SIDE + PIXELS : PADDED, :] = edge


def put(pad, piece, values):
    column = lax.broadcasted_iota(jnp.int32, values.shape, 0) % SIDE
    left = jnp.where(column == 0, 0.0, pltpu.roll(values, 1, 0))
    right = jnp.where(column == SIDE - 1, 0.0, pltpu.roll(values, PIECE - 1, 0))
    rows = pl.ds(SIDE + piece * PIECE, PIECE)
    pad[rows, 0:CHANNELS] = left.astype(LOW)
    pad[rows, CHANNELS : 2 * CHANNELS] = values.astype(LOW)
    pad[rows, 2 * CHANNELS : 3 * CHANNELS] = right.astype(LOW)


def put_active(pad, state):
    for piece in range(PIXELS // PIECE):
        put(pad, piece, jnp.tanh(state[pl.ds(piece * PIECE, PIECE), :]))


def conv(pad, kernel, chunk):
    columns = jnp.concatenate(
        [pad[pl.ds(chunk * CHUNK + SIDE * shift, CHUNK), :] for shift in range(3)], axis=1
    )
    return jnp.dot(columns, kernel[...], preferred_element_type=FULL)


def chunks():
    return [(chunk, pl.ds(chunk * CHUNK, CHUNK)) for chunk in range(PIXELS // CHUNK)]


def relax_kernel(begin, weights, out, state, pad):
    clear(pad)
    state[...] = begin[...]

    def step(layer, carry):
        put_active(pad, state)
        for chunk, rows in chunks():
            state[rows, :] += STEP_SIZE * conv(pad, weights.at[layer], chunk)
        return carry

    lax.fori_loop(0, SECTION, step, 0)
    out[...] = state[...]


def fine_kernel(place, own, received, weights, closing, defect_out, send_out, state, base, first, pad):
    section, phase = place[0], place[1]
    clear(pad)
    for _, rows in chunks():
        begin = jnp.where(section == 0, own[rows, :], received[rows, :])
        state[rows, :] = begin
        base[rows, :] = begin

    put_active(pad, state)
    for chunk, rows in chunks():
        term = conv(pad, weights.at[0], chunk)
        first[rows, :] = term
        state[rows, :] += STEP_SIZE * term

    @pl.when(phase == 0)
    def _():
        for chunk, rows in chunks():
            long_term = (4 * SECTION * STEP_SIZE) * conv(pad, closing.at[SECTION - 1], chunk)
            base[rows, :] += long_term

    def step(layer, carry):
        put_active(pad, state)
        for chunk, rows in chunks():
            state[rows, :] += STEP_SIZE * conv(pad, weights.at[layer], chunk)
        return carry

    lax.fori_loop(1, SECTION, step, 0)
    for _, rows in chunks():
        begin = jnp.where(section == 0, own[rows, :], received[rows, :])
        last = state[rows, :]
        defect = (last - begin) - SECTION * STEP_SIZE * first[rows, :]
        defect_out[rows, :] = defect.astype(LOW)
        send_out[0, rows, :] = jnp.where(phase == 0, last, defect)
        total = jnp.where(section == 0, begin, last - base[rows, :])
        send_out[1, rows, :] = jnp.where(phase == 0, total, defect)


def first_round_kernel(place, sent, received, leading, out, state, pad):
    phase, in_first_group = place[1], place[0] < 4

    @pl.when(phase < 2)
    def _():
        clear(pad)
        for _, rows in chunks():
            state[rows, :] = jnp.where(phase == 0, sent[0, rows, :], received[0, rows, :])
        put_active(pad, state)
        for chunk, rows in chunks():
            defect = jnp.where(phase == 0, received[0, rows, :], sent[0, rows, :])
            total = jnp.where(phase == 0, sent[1, rows, :], received[1, rows, :])
            change = SECTION * STEP_SIZE * conv(pad, leading.at[1], chunk) + defect
            out[0, rows, :] = state[rows, :] + change
            out[1, rows, :] = total + jnp.where(in_first_group, 0.0, change)

    @pl.when(phase >= 2)
    def _():
        for _, rows in chunks():
            out[0, rows, :] = jnp.where(phase == 2, sent[0, rows, :], received[0, rows, :])
            out[1, rows, :] = jnp.where(phase == 2, received[0, rows, :], sent[0, rows, :])


def closing_kernel(place, sent, received, leading, out, total, state, pad):
    phase, in_first_group = place[1], place[0] < 4
    clear(pad)
    for _, rows in chunks():
        state[rows, :] = jnp.where(phase < 2, sent[0, rows, :], received[0, rows, :])
        total[rows, :] = jnp.where(phase < 2, sent[1, rows, :], received[1, rows, :])

    def step(turn, carry):
        put_active(pad, state)
        for chunk, rows in chunks():
            defect = jnp.where(phase < 2, received[turn, rows, :], sent[turn, rows, :])
            change = SECTION * STEP_SIZE * conv(pad, leading.at[2 + turn], chunk) + defect
            state[rows, :] += change
            total[rows, :] += jnp.where(in_first_group, 0.0, change)
        return carry

    lax.fori_loop(0, 2, step, 0)
    for _, rows in chunks():
        out[rows, :] = jnp.where(in_first_group, state[rows, :], total[rows, :])


def load(sources, targets, arrived):
    copies = [
        pltpu.make_async_copy(source, target, arrived.at[number])
        for number, (source, target) in enumerate(zip(sources, targets))
    ]
    for copy in copies:
        copy.start()
    return copies


def final_kernel(place, *refs):
    stored, out, refs = refs[:15], refs[15], refs[16:]
    state, begin, end, slopes, change, pads, back_pad, grads, slots = refs[:9]
    held, arrived = refs[9:16], refs[16]
    coarse, images, defects, leading, weights, flipped, end_adjoint = held
    phase, group, replica = place[1], place[2], place[3]
    copies = load(stored, [slots.at[number] for number in range(8)] + list(held), arrived)
    clear(back_pad)
    for layer in range(SECTION):
        clear(pads.at[layer])
    grads[3 * CHANNELS :, :] = jnp.zeros((8, CHANNELS), FULL)

    for copy in copies[:10]:
        copy.wait()
    for _, rows in chunks():
        state[rows, :] = slots[group, rows, :]

    def chain_step(turn, carry):
        put_active(back_pad, state)
        for chunk, rows in chunks():
            long_term = (4 * SECTION * STEP_SIZE) * conv(back_pad, coarse.at[turn], chunk)
            state[rows, :] += long_term + slots[group - turn, rows, :]
        return carry

    lax.fori_loop(1, group, chain_step, 0)
    for _, rows in chunks():
        begin[rows, :] = jnp.where(group == 0, images[rows, :], state[rows, :])

    @pl.when(group > 0)
    def _():
        chain_step(group, 0)

    for _, rows in chunks():
        end[rows, :] = state[rows, :]
        state[rows, :] = begin[rows, :]
    for copy in copies[10:12]:
        copy.wait()

    def level_step(turn, carry):
        put_active(back_pad, state)
        for chunk, rows in chunks():
            state[rows, :] += (
                SECTION * STEP_SIZE * conv(back_pad, leading.at[turn], chunk)
                + defects[turn, rows, :].astype(FULL)
            )

        @pl.when(phase == turn)
        def _():
            end[...] = state[...]

        @pl.when(phase == turn + 1)
        def _():
            begin[...] = state[...]

        return carry

    lax.fori_loop(0, 3, level_step, 0)
    for copy in copies[12:]:
        copy.wait()

    def active(layer):
        for piece in range(PIXELS // PIECE):
            rows = pl.ds(piece * PIECE, PIECE)
            slope = jnp.tanh(begin[rows, :])
            slopes[layer, rows, :] = STEP_SIZE * (1.0 - slope * slope)
            put(pads.at[layer], piece, slope)

    def forward(layer, carry):
        active(layer)
        for chunk, rows in chunks():
            begin[rows, :] += STEP_SIZE * conv(pads.at[layer], weights.at[layer], chunk)
        return carry

    lax.fori_loop(0, SECTION - 1, forward, 0)
    active(SECTION - 1)
    change[...] = jnp.zeros(IMAGE, FULL)

    def backward(turn, carry):
        layer = SECTION - 1 - turn
        for piece in range(PIXELS // PIECE):
            rows = pl.ds(piece * PIECE, PIECE)
            put(back_pad, piece, end_adjoint[rows, :] + change[rows, :])
        low = back_pad[pl.ds(SIDE, PIXELS), CHANNELS : 2 * CHANNELS]
        for part in range(3):
            offset = 2 * replica + part
            columns = pads[
                layer,
                pl.ds(pl.multiple_of(SIDE * (offset // 3), SIDE), PIXELS),
                pl.ds(pl.multiple_of(CHANNELS * (offset % 3), CHANNELS), CHANNELS),
            ]
            grads[pl.ds(part * CHANNELS, CHANNELS), :] = STEP_SIZE * lax.dot_general(
                columns, low, (((0,), (0,)), ((), ())), preferred_element_type=FULL
            )
        for block in range(4):
            rows = pl.ds(pl.multiple_of(SIDE * replica + 72 * block, 8), 80)
            out[block, pl.ds(pl.multiple_of(192 + 80 * layer, 16), 80), :] = grads[rows, :].astype(LOW)
        for chunk, rows in chunks():
            change[rows, :] += slopes[layer, rows, :] * conv(back_pad, flipped.at[layer], chunk)
        return carry

    lax.fori_loop(0, SECTION, backward, 0)
    for block in range(4):
        kept = pl.ds(pl.multiple_of(replica * 256 + block * 64, 64), 64)
        high = end[kept, :].astype(LOW)
        out[block, 0:64, :] = high
        out[block, 64:128, :] = (end[kept, :] - high.astype(FULL)).astype(LOW)
        out[block, 128:192, :] = change[kept, :].astype(LOW)


def call(body, outs, scratch, megabytes, place, *operands, stored=()):
    held = pl.BlockSpec(memory_space=pltpu.VMEM)
    in_specs = [held] * len(operands) + [pl.BlockSpec(memory_space=pltpu.HBM)] * len(stored)
    operands += tuple(stored)
    if place is not None:
        in_specs = [pl.BlockSpec(memory_space=pltpu.SMEM)] + in_specs
        operands = (place,) + operands
    return pl.pallas_call(
        body,
        out_shape=outs,
        in_specs=in_specs,
        out_specs=jax.tree.map(lambda _: held, outs),
        scratch_shapes=scratch,
        compiler_params=pltpu.CompilerParams(vmem_limit_bytes=megabytes * 1024 * 1024),
    )(*operands)


def shape(*dims, dtype=FULL):
    return jax.ShapeDtypeStruct(dims, dtype)


def wide():
    return pltpu.VMEM(IMAGE, FULL)


def padding():
    return pltpu.VMEM(PAD_SCRATCH, LOW)


def swap(block, distance, sections):
    moved = lax.ppermute(block.astype(SENT), "layer", [(i, i ^ distance) for i in range(sections)])
    return moved.astype(block.dtype)


def shift(block, distance, sections):
    route = [(i, i + distance) for i in range(sections - distance)]
    return lax.ppermute(block.astype(SENT), "layer", route).astype(block.dtype)


def local(images, end_guess, end_adjoint, weights):
    section = lax.axis_index("layer")
    tile = lax.axis_index("space")
    sections = lax.axis_size("layer")
    tiles = lax.axis_size("space")
    replica = tile // 4
    group = section // 4
    place = jnp.stack([section, section % 4, group, replica]).astype(jnp.int32)
    rows_of_groups = [[4 * g + i for i in range(4)] for g in range(sections // 4)]
    columns_of_groups = [[4 * g + i for g in range(sections // 4)] for i in range(4)]

    guess, leading = lax.optimization_barrier((end_guess[0].astype(SENT), weights[0]))
    leading = lax.all_gather(leading, "layer", axis_index_groups=rows_of_groups)
    guess = jnp.where(section == 0, images, shift(guess, 1, sections).astype(FULL))
    both = jnp.stack([guess, end_adjoint[0]], axis=1).astype(SENT)
    both = lax.all_to_all(jnp.tile(both, (tiles // 4, 1, 1, 1, 1)), "space", 0, 0, tiled=True)
    both = both.astype(FULL)
    start, adjoint_whole = both[:, 0].reshape(IMAGE), both[:, 1].reshape(IMAGE)

    flipped = (
        weights.reshape(SECTION, 9, CHANNELS, CHANNELS)[:, ::-1]
        .transpose(0, 1, 3, 2)
        .reshape(SECTION, 9 * CHANNELS, CHANNELS)
    )
    image_shape, pair_shape = shape(*IMAGE), shape(2, *IMAGE)

    relaxed = call(relax_kernel, image_shape, [wide(), padding()], 8, None, start, weights)
    closing_weights, _ = lax.optimization_barrier((leading[3], relaxed))
    received = shift(relaxed, 1, sections)
    coarse = lax.all_gather(closing_weights, "layer", axis_index_groups=columns_of_groups)
    defect, send = call(
        fine_kernel,
        (shape(*IMAGE, dtype=LOW), pair_shape),
        [wide(), wide(), wide(), padding()],
        12, place, start, received, weights, leading,
    )
    defects = lax.all_gather(defect, "layer", axis_index_groups=rows_of_groups)
    received = swap(send, 1, sections)
    send = call(first_round_kernel, pair_shape, [wide(), padding()], 10, place, send, received, leading)
    received = swap(send, 3, sections)
    defect_two, base = call(
        closing_kernel, (image_shape, image_shape), [wide(), padding()], 10, place, send, received, leading
    )
    up = [(i, (i + 4) % sections) for i in range(sections)]
    down = [(j, i) for i, j in up]
    ups, downs, widened = [defect_two.astype(SENT)], [defect_two.astype(SENT)], {}
    for turn in range(4):
        moved = [lax.ppermute(ups[-1], "layer", up)]
        if turn < 3:
            moved.append(lax.ppermute(downs[-1], "layer", down))
        if turn:
            ready = [ups[-1].astype(FULL), downs[-1].astype(FULL)]
            moved, (widened[turn], widened[8 - turn]) = lax.optimization_barrier((moved, ready))
        ups.append(moved[0])
        if turn < 3:
            downs.append(moved[1])
    widened[4], coarse = lax.optimization_barrier((ups[-1], coarse))
    slots = [defect_two] + [widened[distance].astype(FULL) for distance in range(1, 8)]
    stored = (coarse, base, defects, leading, weights, flipped, adjoint_whole)
    parts = call(
        final_kernel,
        shape(4, 512, CHANNELS, dtype=LOW),
        [
            wide(), wide(), wide(),
            pltpu.VMEM((SECTION, *IMAGE), FULL),
            wide(),
            pltpu.VMEM((SECTION, *PAD_SCRATCH), LOW),
            padding(),
            pltpu.VMEM((3 * CHANNELS + 8, CHANNELS), FULL),
            pltpu.VMEM((8, *IMAGE), FULL),
            *[pltpu.VMEM(array.shape, array.dtype) for array in stored],
            pltpu.SemaphoreType.DMA((8 + len(stored),)),
        ],
        60, place, stored=(*slots, *stored),
    )
    row_groups = [[4 * r + n for n in range(4)] for r in range(tiles // 4)]
    parts = lax.all_to_all(parts, "space", 0, 0, axis_index_groups=row_groups, tiled=True).astype(FULL)
    tile_shape = (1, 4, 2, SIDE, CHANNELS)
    section_ends = (parts[:, 0:64] + parts[:, 64:128]).reshape(tile_shape)
    start_adjoint = end_adjoint + parts[:, 128:192].reshape(tile_shape)
    weight_grad = parts[:, 192:].sum(0).reshape(SECTION, 80, CHANNELS)[:, :72]
    return section_ends, start_adjoint, weight_grad


def solution(mesh):
    return jax.shard_map(
        local,
        mesh=mesh,
        in_specs=(
            P(None, "space", None, None),
            P("layer", None, "space", None, None),
            P("layer", None, "space", None, None),
            P("layer", None, None),
        ),
        out_specs=(
            P("layer", None, "space", None, None),
            P("layer", None, "space", None, None),
            P("layer", "space", None),
        ),
        check_vma=False,
    )
```

```python
import jax
import jax.numpy as jnp
from jax import lax
from jax.experimental import pallas as pl
from jax.experimental.pallas import tpu as pltpu
from jax.sharding import PartitionSpec as P

STEP_SIZE = 0.1
SECTION = 4
SIDE = 32
CHANNELS = 128
PIXELS = SIDE * SIDE
PADDED = PIXELS + 2 * SIDE
PIECE = 128
CHUNK = 256
LOW = jnp.bfloat16
FULL = jnp.float32
SENT = jnp.float16

IMAGE = (PIXELS, CHANNELS)
PAD_SCRATCH = (PADDED, 3 * CHANNELS)


def clear(pad):
    edge = jnp.zeros((SIDE, 3 * CHANNELS), LOW)
    pad[0:SIDE, :] = edge
    pad[SIDE + PIXELS : PADDED, :] = edge


def put(pad, piece, values):
    column = lax.broadcasted_iota(jnp.int32, values.shape, 0) % SIDE
    left = jnp.where(column == 0, 0.0, pltpu.roll(values, 1, 0))
    right = jnp.where(column == SIDE - 1, 0.0, pltpu.roll(values, PIECE - 1, 0))
    rows = pl.ds(SIDE + piece * PIECE, PIECE)
    pad[rows, 0:CHANNELS] = left.astype(LOW)
    pad[rows, CHANNELS : 2 * CHANNELS] = values.astype(LOW)
    pad[rows, 2 * CHANNELS : 3 * CHANNELS] = right.astype(LOW)


def put_active(pad, state):
    for piece in range(PIXELS // PIECE):
        put(pad, piece, jnp.tanh(state[pl.ds(piece * PIECE, PIECE), :]))


def conv(pad, kernel, chunk):
    columns = jnp.concatenate(
        [pad[pl.ds(chunk * CHUNK + SIDE * shift, CHUNK), :] for shift in range(3)], axis=1
    )
    return jnp.dot(columns, kernel[...], preferred_element_type=FULL)


def chunks():
    return [(chunk, pl.ds(chunk * CHUNK, CHUNK)) for chunk in range(PIXELS // CHUNK)]


def relax_kernel(begin, weights, out, state, pad):
    clear(pad)
    state[...] = begin[...]

    def step(layer, carry):
        put_active(pad, state)
        for chunk, rows in chunks():
            state[rows, :] += STEP_SIZE * conv(pad, weights.at[layer], chunk)
        return carry

    lax.fori_loop(0, SECTION, step, 0)
    out[...] = state[...]


def fine_kernel(place, own, received, weights, closing, defect_out, first_out, second_out, state, base, first, pad):
    section, phase = place[0], place[1]
    clear(pad)
    for _, rows in chunks():
        begin = jnp.where(section == 0, own[rows, :], received[rows, :])
        state[rows, :] = begin
        base[rows, :] = begin

    put_active(pad, state)
    for chunk, rows in chunks():
        term = conv(pad, weights.at[0], chunk)
        first[rows, :] = term
        state[rows, :] += STEP_SIZE * term

    @pl.when(phase == 0)
    def _():
        for chunk, rows in chunks():
            long_term = (4 * SECTION * STEP_SIZE) * conv(pad, closing.at[SECTION - 1], chunk)
            base[rows, :] += long_term

    def step(layer, carry):
        put_active(pad, state)
        for chunk, rows in chunks():
            state[rows, :] += STEP_SIZE * conv(pad, weights.at[layer], chunk)
        return carry

    lax.fori_loop(1, SECTION, step, 0)
    for _, rows in chunks():
        begin = jnp.where(section == 0, own[rows, :], received[rows, :])
        last = state[rows, :]
        defect = (last - begin) - SECTION * STEP_SIZE * first[rows, :]
        defect_out[rows, :] = defect.astype(LOW)
        first_out[rows, :] = jnp.where(phase == 0, last, defect)
        coarse_part = jnp.where(section == 0, begin, -base[rows, :])
        second_out[rows, :] = jnp.where(phase == 0, coarse_part, defect)


def first_round_kernel(place, mine, coarse_part, near, across, leading, near_out, across_out, state, pad):
    phase = place[1]

    @pl.when(phase < 2)
    def _():
        clear(pad)
        for _, rows in chunks():
            state[rows, :] = jnp.where(phase == 0, mine[rows, :], near[rows, :])
        put_active(pad, state)
        for chunk, rows in chunks():
            defect = jnp.where(phase == 0, near[rows, :], mine[rows, :])
            state[rows, :] += SECTION * STEP_SIZE * conv(pad, leading.at[1], chunk) + defect
            across_out[rows, :] = state[rows, :]
            near_out[rows, :] = coarse_part[rows, :]

    @pl.when(phase == 1)
    def _():
        put_active(pad, state)
        for chunk, rows in chunks():
            change = SECTION * STEP_SIZE * conv(pad, leading.at[2], chunk) + across[rows, :]
            near_out[rows, :] = state[rows, :] + change

    @pl.when(phase >= 2)
    def _():
        for _, rows in chunks():
            near_out[rows, :] = jnp.where(phase == 3, across[rows, :], near[rows, :])
            across_out[rows, :] = near[rows, :]


def closing_kernel(
    place, mine, coarse_part, near, across, level, near_later, across_later, leading, out, base, state, pad
):
    phase, in_first_group = place[1], place[0] < 4
    clear(pad)

    @pl.when(phase < 2)
    def _():
        for _, rows in chunks():
            state[rows, :] = jnp.where(phase == 0, near_later[rows, :], level[rows, :])
            base[rows, :] = jnp.where(phase == 0, coarse_part[rows, :], near_later[rows, :])
            out[rows, :] = jnp.where(phase == 0, across[rows, :], across_later[rows, :])

    @pl.when(phase >= 2)
    def _():
        for _, rows in chunks():
            state[rows, :] = across_later[rows, :]
            base[rows, :] = jnp.where(phase == 2, near_later[rows, :], across[rows, :])
            out[rows, :] = jnp.where(phase == 2, near[rows, :], mine[rows, :])
        put_active(pad, state)
        for chunk, rows in chunks():
            defect = jnp.where(phase == 2, mine[rows, :], near[rows, :])
            state[rows, :] += SECTION * STEP_SIZE * conv(pad, leading.at[2], chunk) + defect

    put_active(pad, state)
    for chunk, rows in chunks():
        closing = state[rows, :] + SECTION * STEP_SIZE * conv(pad, leading.at[3], chunk) + out[rows, :]
        out[rows, :] = closing + jnp.where(in_first_group, 0.0, base[rows, :])


def load(sources, targets, arrived):
    copies = [
        pltpu.make_async_copy(source, target, arrived.at[number])
        for number, (source, target) in enumerate(zip(sources, targets))
    ]
    for copy in copies:
        copy.start()
    return copies


def final_kernel(place, *refs):
    stored, out, refs = refs[:15], refs[15], refs[16:]
    state, begin, end, slopes, change, pads, back_pad, grads, slots = refs[:9]
    held, arrived = refs[9:16], refs[16]
    coarse, images, defects, leading, weights, flipped, end_adjoint = held
    phase, group, replica = place[1], place[2], place[3]
    copies = load(stored, [slots.at[number] for number in range(8)] + list(held), arrived)
    clear(back_pad)
    for layer in range(SECTION):
        clear(pads.at[layer])
    grads[3 * CHANNELS :, :] = jnp.zeros((8, CHANNELS), FULL)

    for copy in copies[:10]:
        copy.wait()
    for _, rows in chunks():
        state[rows, :] = slots[group, rows, :]

    def chain_step(turn, carry):
        put_active(back_pad, state)
        for chunk, rows in chunks():
            long_term = (4 * SECTION * STEP_SIZE) * conv(back_pad, coarse.at[turn], chunk)
            state[rows, :] += long_term + slots[group - turn, rows, :]
        return carry

    lax.fori_loop(1, group, chain_step, 0)
    for _, rows in chunks():
        begin[rows, :] = jnp.where(group == 0, images[rows, :], state[rows, :])

    @pl.when(group > 0)
    def _():
        chain_step(group, 0)

    for _, rows in chunks():
        end[rows, :] = state[rows, :]
        state[rows, :] = begin[rows, :]
    for copy in copies[10:12]:
        copy.wait()

    def level_step(turn, carry):
        put_active(back_pad, state)
        for chunk, rows in chunks():
            state[rows, :] += (
                SECTION * STEP_SIZE * conv(back_pad, leading.at[turn], chunk)
                + defects[turn, rows, :].astype(FULL)
            )

        @pl.when(phase == turn)
        def _():
            end[...] = state[...]

        @pl.when(phase == turn + 1)
        def _():
            begin[...] = state[...]

        return carry

    lax.fori_loop(0, 3, level_step, 0)
    for copy in copies[12:]:
        copy.wait()

    def active(layer):
        for piece in range(PIXELS // PIECE):
            rows = pl.ds(piece * PIECE, PIECE)
            slope = jnp.tanh(begin[rows, :])
            slopes[layer, rows, :] = STEP_SIZE * (1.0 - slope * slope)
            put(pads.at[layer], piece, slope)

    def forward(layer, carry):
        active(layer)
        for chunk, rows in chunks():
            begin[rows, :] += STEP_SIZE * conv(pads.at[layer], weights.at[layer], chunk)
        return carry

    lax.fori_loop(0, SECTION - 1, forward, 0)
    active(SECTION - 1)
    change[...] = jnp.zeros(IMAGE, FULL)

    def backward(turn, carry):
        layer = SECTION - 1 - turn
        for piece in range(PIXELS // PIECE):
            rows = pl.ds(piece * PIECE, PIECE)
            put(back_pad, piece, end_adjoint[rows, :] + change[rows, :])
        low = back_pad[pl.ds(SIDE, PIXELS), CHANNELS : 2 * CHANNELS].T
        for part in range(3):
            offset = 2 * replica + part
            columns = pads[
                layer,
                pl.ds(pl.multiple_of(SIDE * (offset // 3), SIDE), PIXELS),
                pl.ds(pl.multiple_of(CHANNELS * (offset % 3), CHANNELS), CHANNELS),
            ]
            term = jnp.dot(low, columns, preferred_element_type=FULL)
            grads[pl.ds(part * CHANNELS, CHANNELS), :] = STEP_SIZE * term.T
        for block in range(4):
            rows = pl.ds(pl.multiple_of(SIDE * replica + 72 * block, 8), 80)
            out[block, pl.ds(pl.multiple_of(192 + 80 * layer, 16), 80), :] = grads[rows, :].astype(LOW)
        for chunk, rows in chunks():
            change[rows, :] += slopes[layer, rows, :] * conv(back_pad, flipped.at[layer], chunk)
        return carry

    lax.fori_loop(0, SECTION, backward, 0)
    for block in range(4):
        kept = pl.ds(pl.multiple_of(replica * 256 + block * 64, 64), 64)
        high = end[kept, :].astype(LOW)
        out[block, 0:64, :] = high
        out[block, 64:128, :] = (end[kept, :] - high.astype(FULL)).astype(LOW)
        out[block, 128:192, :] = change[kept, :].astype(LOW)


def call(body, outs, scratch, megabytes, place, *operands, stored=()):
    held = pl.BlockSpec(memory_space=pltpu.VMEM)
    in_specs = [held] * len(operands) + [pl.BlockSpec(memory_space=pltpu.HBM)] * len(stored)
    operands += tuple(stored)
    if place is not None:
        in_specs = [pl.BlockSpec(memory_space=pltpu.SMEM)] + in_specs
        operands = (place,) + operands
    return pl.pallas_call(
        body,
        out_shape=outs,
        in_specs=in_specs,
        out_specs=jax.tree.map(lambda _: held, outs),
        scratch_shapes=scratch,
        compiler_params=pltpu.CompilerParams(vmem_limit_bytes=megabytes * 1024 * 1024),
    )(*operands)


def shape(*dims, dtype=FULL):
    return jax.ShapeDtypeStruct(dims, dtype)


def wide():
    return pltpu.VMEM(IMAGE, FULL)


def padding():
    return pltpu.VMEM(PAD_SCRATCH, LOW)


def swap(block, distance, sections):
    moved = lax.ppermute(block.astype(SENT), "layer", [(i, i ^ distance) for i in range(sections)])
    return moved.astype(block.dtype)


def shift(block, distance, sections):
    route = [(i, i + distance) for i in range(sections - distance)]
    return lax.ppermute(block.astype(SENT), "layer", route).astype(block.dtype)


def local(images, end_guess, end_adjoint, weights):
    section = lax.axis_index("layer")
    tile = lax.axis_index("space")
    sections = lax.axis_size("layer")
    tiles = lax.axis_size("space")
    replica = tile // 4
    group = section // 4
    place = jnp.stack([section, section % 4, group, replica]).astype(jnp.int32)
    rows_of_groups = [[4 * g + i for i in range(4)] for g in range(sections // 4)]
    columns_of_groups = [[4 * g + i for g in range(sections // 4)] for i in range(4)]

    guess, leading = lax.optimization_barrier((end_guess[0].astype(SENT), weights[0]))
    leading = lax.all_gather(leading, "layer", axis_index_groups=rows_of_groups)
    guess = jnp.where(section == 0, images, shift(guess, 1, sections).astype(FULL))
    both = jnp.stack([guess, end_adjoint[0]], axis=1).astype(SENT)
    both = lax.all_to_all(jnp.tile(both, (tiles // 4, 1, 1, 1, 1)), "space", 0, 0, tiled=True)
    both = both.astype(FULL)
    start, adjoint_whole = both[:, 0].reshape(IMAGE), both[:, 1].reshape(IMAGE)

    flipped = (
        weights.reshape(SECTION, 9, CHANNELS, CHANNELS)[:, ::-1]
        .transpose(0, 1, 3, 2)
        .reshape(SECTION, 9 * CHANNELS, CHANNELS)
    )
    image_shape = shape(*IMAGE)

    relaxed = call(relax_kernel, image_shape, [wide(), padding()], 8, None, start, weights)
    closing_weights, _ = lax.optimization_barrier((leading[3], relaxed))
    received = shift(relaxed, 1, sections)
    coarse = lax.all_gather(closing_weights, "layer", axis_index_groups=columns_of_groups)
    defect, mine, coarse_part = call(
        fine_kernel,
        (shape(*IMAGE, dtype=LOW), image_shape, image_shape),
        [wide(), wide(), wide(), padding()],
        12, place, start, received, weights, leading,
    )
    defects = lax.all_gather(defect, "layer", axis_index_groups=rows_of_groups)
    near, across = swap(mine, 1, sections), swap(coarse_part, 3, sections)
    level, passed = call(
        first_round_kernel, (image_shape, image_shape), [wide(), padding()], 10,
        place, mine, coarse_part, near, across, leading,
    )
    near_later, across_later = swap(level, 1, sections), swap(passed, 3, sections)
    defect_two, base = call(
        closing_kernel, (image_shape, image_shape), [wide(), padding()], 12,
        place, mine, coarse_part, near, across, level, near_later, across_later, leading,
    )
    up = [(i, (i + 4) % sections) for i in range(sections)]
    down = [(j, i) for i, j in up]
    ups, downs, widened = [defect_two.astype(SENT)], [defect_two.astype(SENT)], {}
    for turn in range(4):
        moved = [lax.ppermute(ups[-1], "layer", up)]
        if turn < 3:
            moved.append(lax.ppermute(downs[-1], "layer", down))
        if turn:
            ready = [ups[-1].astype(FULL), downs[-1].astype(FULL)]
            moved, (widened[turn], widened[8 - turn]) = lax.optimization_barrier((moved, ready))
        ups.append(moved[0])
        if turn < 3:
            downs.append(moved[1])
    widened[4], coarse = lax.optimization_barrier((ups[-1], coarse))
    slots = [defect_two] + [widened[distance].astype(FULL) for distance in range(1, 8)]
    stored = (coarse, base, defects, leading, weights, flipped, adjoint_whole)
    parts = call(
        final_kernel,
        shape(4, 512, CHANNELS, dtype=LOW),
        [
            wide(), wide(), wide(),
            pltpu.VMEM((SECTION, *IMAGE), FULL),
            wide(),
            pltpu.VMEM((SECTION, *PAD_SCRATCH), LOW),
            padding(),
            pltpu.VMEM((3 * CHANNELS + 8, CHANNELS), FULL),
            pltpu.VMEM((8, *IMAGE), FULL),
            *[pltpu.VMEM(array.shape, array.dtype) for array in stored],
            pltpu.SemaphoreType.DMA((8 + len(stored),)),
        ],
        60, place, stored=(*slots, *stored),
    )
    row_groups = [[4 * r + n for n in range(4)] for r in range(tiles // 4)]
    parts = lax.all_to_all(parts, "space", 0, 0, axis_index_groups=row_groups, tiled=True).astype(FULL)
    tile_shape = (1, 4, 2, SIDE, CHANNELS)
    section_ends = (parts[:, 0:64] + parts[:, 64:128]).reshape(tile_shape)
    start_adjoint = end_adjoint + parts[:, 128:192].reshape(tile_shape)
    weight_grad = parts[:, 192:].sum(0).reshape(SECTION, 80, CHANNELS)[:, :72]
    return section_ends, start_adjoint, weight_grad


def solution(mesh):
    return jax.shard_map(
        local,
        mesh=mesh,
        in_specs=(
            P(None, "space", None, None),
            P("layer", None, "space", None, None),
            P("layer", None, "space", None, None),
            P("layer", None, None),
        ),
        out_specs=(
            P("layer", None, "space", None, None),
            P("layer", None, "space", None, None),
            P("layer", "space", None),
        ),
        check_vma=False,
    )
```

```python
import jax
import jax.numpy as jnp
from jax import lax
from jax.experimental import pallas as pl
from jax.experimental.pallas import tpu as pltpu
from jax.sharding import PartitionSpec as P

STEP_SIZE = 0.1
SECTION = 4
SIDE = 32
CHANNELS = 128
PIXELS = SIDE * SIDE
PADDED = PIXELS + 2 * SIDE
PIECE = 128
CHUNK = 256
LOW = jnp.bfloat16
FULL = jnp.float32
SENT = jnp.float16

IMAGE = (PIXELS, CHANNELS)
PAD_SCRATCH = (PADDED, 3 * CHANNELS)


def clear(pad):
    edge = jnp.zeros((SIDE, 3 * CHANNELS), LOW)
    pad[0:SIDE, :] = edge
    pad[SIDE + PIXELS : PADDED, :] = edge


def put(pad, piece, values):
    column = lax.broadcasted_iota(jnp.int32, values.shape, 0) % SIDE
    left = jnp.where(column == 0, 0.0, pltpu.roll(values, 1, 0))
    right = jnp.where(column == SIDE - 1, 0.0, pltpu.roll(values, PIECE - 1, 0))
    rows = pl.ds(SIDE + piece * PIECE, PIECE)
    pad[rows, 0:CHANNELS] = left.astype(LOW)
    pad[rows, CHANNELS : 2 * CHANNELS] = values.astype(LOW)
    pad[rows, 2 * CHANNELS : 3 * CHANNELS] = right.astype(LOW)


def conv(pad, kernel, chunk):
    columns = jnp.concatenate(
        [pad[pl.ds(chunk * CHUNK + SIDE * shift, CHUNK), :] for shift in range(3)], axis=1
    )
    return jnp.dot(columns, kernel[...], preferred_element_type=FULL)


def chunks():
    return [(chunk, pl.ds(chunk * CHUNK, CHUNK)) for chunk in range(PIXELS // CHUNK)]


def swept(pad, state, put_piece=None):
    done = 0
    for chunk, rows in chunks():
        while done < min(2 * chunk + 3, PIXELS // PIECE):
            if put_piece is None:
                put(pad, done, jnp.tanh(state[pl.ds(done * PIECE, PIECE), :]))
            else:
                put_piece(done)
            done += 1
        yield chunk, rows


def relax_kernel(begin, weights, out, state, pad):
    clear(pad)
    state[...] = begin[...]

    def step(layer, carry):
        for chunk, rows in swept(pad, state):
            state[rows, :] += STEP_SIZE * conv(pad, weights.at[layer], chunk)
        return carry

    lax.fori_loop(0, SECTION, step, 0)
    out[...] = state[...]


def fine_kernel(place, own, received, weights, closing, defect_out, first_out, second_out, state, base, first, pad):
    section, phase = place[0], place[1]
    clear(pad)
    for _, rows in chunks():
        begin = jnp.where(section == 0, own[rows, :], received[rows, :])
        state[rows, :] = begin
        base[rows, :] = begin

    for chunk, rows in swept(pad, state):
        term = conv(pad, weights.at[0], chunk)
        first[rows, :] = term
        state[rows, :] += STEP_SIZE * term

    @pl.when(phase == 0)
    def _():
        for chunk, rows in chunks():
            long_term = (4 * SECTION * STEP_SIZE) * conv(pad, closing.at[SECTION - 1], chunk)
            base[rows, :] += long_term

    def step(layer, carry):
        for chunk, rows in swept(pad, state):
            state[rows, :] += STEP_SIZE * conv(pad, weights.at[layer], chunk)
        return carry

    lax.fori_loop(1, SECTION, step, 0)
    for _, rows in chunks():
        begin = jnp.where(section == 0, own[rows, :], received[rows, :])
        last = state[rows, :]
        defect = (last - begin) - SECTION * STEP_SIZE * first[rows, :]
        defect_out[rows, :] = defect.astype(LOW)
        first_out[rows, :] = jnp.where(phase == 0, last, defect)
        coarse_part = jnp.where(section == 0, begin, -base[rows, :])
        second_out[rows, :] = jnp.where(phase == 0, coarse_part, defect)


def first_round_kernel(place, mine, coarse_part, near, across, leading, near_out, across_out, state, pad):
    phase = place[1]

    @pl.when(phase < 2)
    def _():
        clear(pad)
        for _, rows in chunks():
            state[rows, :] = jnp.where(phase == 0, mine[rows, :], near[rows, :])
        for chunk, rows in swept(pad, state):
            defect = jnp.where(phase == 0, near[rows, :], mine[rows, :])
            state[rows, :] += SECTION * STEP_SIZE * conv(pad, leading.at[1], chunk) + defect
            across_out[rows, :] = state[rows, :]
            near_out[rows, :] = coarse_part[rows, :]

    @pl.when(phase == 1)
    def _():
        for chunk, rows in swept(pad, state):
            change = SECTION * STEP_SIZE * conv(pad, leading.at[2], chunk) + across[rows, :]
            near_out[rows, :] = state[rows, :] + change

    @pl.when(phase >= 2)
    def _():
        for _, rows in chunks():
            near_out[rows, :] = jnp.where(phase == 3, across[rows, :], near[rows, :])
            across_out[rows, :] = near[rows, :]


def closing_kernel(
    place, mine, coarse_part, near, across, level, near_later, across_later, leading, out, base, state, pad
):
    phase, in_first_group = place[1], place[0] < 4
    clear(pad)

    @pl.when(phase < 2)
    def _():
        for _, rows in chunks():
            state[rows, :] = jnp.where(phase == 0, near_later[rows, :], level[rows, :])
            base[rows, :] = jnp.where(phase == 0, coarse_part[rows, :], near_later[rows, :])
            out[rows, :] = jnp.where(phase == 0, across[rows, :], across_later[rows, :])

    @pl.when(phase >= 2)
    def _():
        for _, rows in chunks():
            state[rows, :] = across_later[rows, :]
            base[rows, :] = jnp.where(phase == 2, near_later[rows, :], across[rows, :])
            out[rows, :] = jnp.where(phase == 2, near[rows, :], mine[rows, :])
        for chunk, rows in swept(pad, state):
            defect = jnp.where(phase == 2, mine[rows, :], near[rows, :])
            state[rows, :] += SECTION * STEP_SIZE * conv(pad, leading.at[2], chunk) + defect

    for chunk, rows in swept(pad, state):
        closing = state[rows, :] + SECTION * STEP_SIZE * conv(pad, leading.at[3], chunk) + out[rows, :]
        out[rows, :] = closing + jnp.where(in_first_group, 0.0, base[rows, :])


def load(sources, targets, arrived):
    copies = [
        pltpu.make_async_copy(source, target, arrived.at[number])
        for number, (source, target) in enumerate(zip(sources, targets))
    ]
    for copy in copies:
        copy.start()
    return copies


def final_kernel(place, *refs):
    stored, out, refs = refs[:15], refs[15], refs[16:]
    state, begin, end, slopes, change, pads, back_pad, grads, slots = refs[:9]
    held, arrived = refs[9:16], refs[16]
    coarse, images, defects, leading, weights, flipped, end_adjoint = held
    phase, group, replica = place[1], place[2], place[3]
    copies = load(stored[:10], [slots.at[number] for number in range(8)] + list(held[:2]), arrived)
    clear(back_pad)
    for layer in range(SECTION):
        clear(pads.at[layer])
    grads[3 * CHANNELS :, :] = jnp.zeros((8, CHANNELS), FULL)

    for copy in copies:
        copy.wait()
    copies = load(stored[10:], held[2:], arrived)
    for _, rows in chunks():
        state[rows, :] = slots[group, rows, :]

    def chain_step(turn, carry):
        for chunk, rows in swept(back_pad, state):
            long_term = (4 * SECTION * STEP_SIZE) * conv(back_pad, coarse.at[turn], chunk)
            state[rows, :] += long_term + slots[group - turn, rows, :]
        return carry

    lax.fori_loop(1, group, chain_step, 0)
    for _, rows in chunks():
        begin[rows, :] = jnp.where(group == 0, images[rows, :], state[rows, :])

    @pl.when(group > 0)
    def _():
        chain_step(group, 0)

    for _, rows in chunks():
        end[rows, :] = state[rows, :]
        state[rows, :] = begin[rows, :]
    for copy in copies[:2]:
        copy.wait()

    def level_step(turn, carry):
        for chunk, rows in swept(back_pad, state):
            state[rows, :] += (
                SECTION * STEP_SIZE * conv(back_pad, leading.at[turn], chunk)
                + defects[turn, rows, :].astype(FULL)
            )

        @pl.when(phase == turn)
        def _():
            end[...] = state[...]

        @pl.when(phase == turn + 1)
        def _():
            begin[...] = state[...]

        return carry

    lax.fori_loop(0, 3, level_step, 0)
    for copy in copies[2:]:
        copy.wait()

    def active(layer, piece):
        rows = pl.ds(piece * PIECE, PIECE)
        slope = jnp.tanh(begin[rows, :])
        slopes[layer, rows, :] = STEP_SIZE * (1.0 - slope * slope)
        put(pads.at[layer], piece, slope)

    def forward(layer, carry):
        for chunk, rows in swept(None, None, lambda piece: active(layer, piece)):
            begin[rows, :] += STEP_SIZE * conv(pads.at[layer], weights.at[layer], chunk)
        return carry

    lax.fori_loop(0, SECTION - 1, forward, 0)
    for piece in range(PIXELS // PIECE):
        active(SECTION - 1, piece)
    change[...] = jnp.zeros(IMAGE, FULL)

    def backward(turn, carry):
        layer = SECTION - 1 - turn
        for piece in range(PIXELS // PIECE):
            rows = pl.ds(piece * PIECE, PIECE)
            put(back_pad, piece, end_adjoint[rows, :] + change[rows, :])
        low = back_pad[pl.ds(SIDE, PIXELS), CHANNELS : 2 * CHANNELS].T
        for part in range(3):
            offset = 2 * replica + part
            columns = pads[
                layer,
                pl.ds(pl.multiple_of(SIDE * (offset // 3), SIDE), PIXELS),
                pl.ds(pl.multiple_of(CHANNELS * (offset % 3), CHANNELS), CHANNELS),
            ]
            term = jnp.dot(low, columns, preferred_element_type=FULL)
            grads[pl.ds(part * CHANNELS, CHANNELS), :] = STEP_SIZE * term.T
        for block in range(4):
            rows = pl.ds(pl.multiple_of(SIDE * replica + 72 * block, 8), 80)
            out[block, pl.ds(pl.multiple_of(192 + 80 * layer, 16), 80), :] = grads[rows, :].astype(LOW)
        for chunk, rows in chunks():
            change[rows, :] += slopes[layer, rows, :] * conv(back_pad, flipped.at[layer], chunk)
        return carry

    lax.fori_loop(0, SECTION, backward, 0)
    for block in range(4):
        kept = pl.ds(pl.multiple_of(replica * 256 + block * 64, 64), 64)
        high = end[kept, :].astype(LOW)
        out[block, 0:64, :] = high
        out[block, 64:128, :] = (end[kept, :] - high.astype(FULL)).astype(LOW)
        out[block, 128:192, :] = change[kept, :].astype(LOW)


def call(body, outs, scratch, megabytes, place, *operands, stored=()):
    held = pl.BlockSpec(memory_space=pltpu.VMEM)
    in_specs = [held] * len(operands) + [pl.BlockSpec(memory_space=pltpu.HBM)] * len(stored)
    operands += tuple(stored)
    if place is not None:
        in_specs = [pl.BlockSpec(memory_space=pltpu.SMEM)] + in_specs
        operands = (place,) + operands
    return pl.pallas_call(
        body,
        out_shape=outs,
        in_specs=in_specs,
        out_specs=jax.tree.map(lambda _: held, outs),
        scratch_shapes=scratch,
        compiler_params=pltpu.CompilerParams(vmem_limit_bytes=megabytes * 1024 * 1024),
    )(*operands)


def shape(*dims, dtype=FULL):
    return jax.ShapeDtypeStruct(dims, dtype)


def wide():
    return pltpu.VMEM(IMAGE, FULL)


def padding():
    return pltpu.VMEM(PAD_SCRATCH, LOW)


def swap(block, distance, sections):
    moved = lax.ppermute(block.astype(SENT), "layer", [(i, i ^ distance) for i in range(sections)])
    return moved.astype(block.dtype)


def shift(block, distance, sections):
    route = [(i, i + distance) for i in range(sections - distance)]
    return lax.ppermute(block.astype(SENT), "layer", route).astype(block.dtype)


def local(images, end_guess, end_adjoint, weights):
    section = lax.axis_index("layer")
    tile = lax.axis_index("space")
    sections = lax.axis_size("layer")
    tiles = lax.axis_size("space")
    replica = tile // 4
    group = section // 4
    place = jnp.stack([section, section % 4, group, replica]).astype(jnp.int32)
    rows_of_groups = [[4 * g + i for i in range(4)] for g in range(sections // 4)]
    columns_of_groups = [[4 * g + i for g in range(sections // 4)] for i in range(4)]

    guess, leading = lax.optimization_barrier((end_guess[0].astype(SENT), weights[0]))
    leading = lax.all_gather(leading, "layer", axis_index_groups=rows_of_groups)
    guess = jnp.where(section == 0, images, shift(guess, 1, sections).astype(FULL))
    both = jnp.stack([guess, end_adjoint[0]], axis=1).astype(SENT)
    both = lax.all_to_all(jnp.tile(both, (tiles // 4, 1, 1, 1, 1)), "space", 0, 0, tiled=True)
    both = both.astype(FULL)
    start, adjoint_whole = both[:, 0].reshape(IMAGE), both[:, 1].reshape(IMAGE)

    flipped = (
        weights.reshape(SECTION, 9, CHANNELS, CHANNELS)[:, ::-1]
        .transpose(0, 1, 3, 2)
        .reshape(SECTION, 9 * CHANNELS, CHANNELS)
    )
    image_shape = shape(*IMAGE)

    relaxed = call(relax_kernel, image_shape, [wide(), padding()], 8, None, start, weights)
    closing_weights, _ = lax.optimization_barrier((leading[3], relaxed))
    received = shift(relaxed, 1, sections)
    coarse = lax.all_gather(closing_weights, "layer", axis_index_groups=columns_of_groups)
    defect, mine, coarse_part = call(
        fine_kernel,
        (shape(*IMAGE, dtype=LOW), image_shape, image_shape),
        [wide(), wide(), wide(), padding()],
        12, place, start, received, weights, leading,
    )
    defects = lax.all_gather(defect, "layer", axis_index_groups=rows_of_groups)
    near, across = swap(mine, 1, sections), swap(coarse_part, 3, sections)
    level, passed = call(
        first_round_kernel, (image_shape, image_shape), [wide(), padding()], 10,
        place, mine, coarse_part, near, across, leading,
    )
    near_later, across_later = swap(level, 1, sections), swap(passed, 3, sections)
    defect_two, base = call(
        closing_kernel, (image_shape, image_shape), [wide(), padding()], 12,
        place, mine, coarse_part, near, across, level, near_later, across_later, leading,
    )
    up = [(i, (i + 4) % sections) for i in range(sections)]
    down = [(j, i) for i, j in up]
    ups, downs, widened = [defect_two.astype(SENT)], [defect_two.astype(SENT)], {}
    for turn in range(4):
        moved = [lax.ppermute(ups[-1], "layer", up)]
        if turn < 3:
            moved.append(lax.ppermute(downs[-1], "layer", down))
        if turn:
            ready = [ups[-1].astype(FULL), downs[-1].astype(FULL)]
            moved, (widened[turn], widened[8 - turn]) = lax.optimization_barrier((moved, ready))
        ups.append(moved[0])
        if turn < 3:
            downs.append(moved[1])
    widened[4], coarse = lax.optimization_barrier((ups[-1], coarse))
    slots = [defect_two] + [widened[distance].astype(FULL) for distance in range(1, 8)]
    stored = (coarse, base, defects, leading, weights, flipped, adjoint_whole)
    parts = call(
        final_kernel,
        shape(4, 512, CHANNELS, dtype=LOW),
        [
            wide(), wide(), wide(),
            pltpu.VMEM((SECTION, *IMAGE), FULL),
            wide(),
            pltpu.VMEM((SECTION, *PAD_SCRATCH), LOW),
            padding(),
            pltpu.VMEM((3 * CHANNELS + 8, CHANNELS), FULL),
            pltpu.VMEM((8, *IMAGE), FULL),
            *[pltpu.VMEM(array.shape, array.dtype) for array in stored],
            pltpu.SemaphoreType.DMA((8 + len(stored),)),
        ],
        60, place, stored=(*slots, *stored),
    )
    row_groups = [[4 * r + n for n in range(4)] for r in range(tiles // 4)]
    parts = lax.all_to_all(parts, "space", 0, 0, axis_index_groups=row_groups, tiled=True).astype(FULL)
    tile_shape = (1, 4, 2, SIDE, CHANNELS)
    section_ends = (parts[:, 0:64] + parts[:, 64:128]).reshape(tile_shape)
    start_adjoint = end_adjoint + parts[:, 128:192].reshape(tile_shape)
    weight_grad = parts[:, 192:].sum(0).reshape(SECTION, 80, CHANNELS)[:, :72]
    return section_ends, start_adjoint, weight_grad


def solution(mesh):
    return jax.shard_map(
        local,
        mesh=mesh,
        in_specs=(
            P(None, "space", None, None),
            P("layer", None, "space", None, None),
            P("layer", None, "space", None, None),
            P("layer", None, None),
        ),
        out_specs=(
            P("layer", None, "space", None, None),
            P("layer", None, "space", None, None),
            P("layer", "space", None),
        ),
        check_vma=False,
    )
```

```python
import jax
import jax.numpy as jnp
from jax import lax
from jax.experimental import pallas as pl
from jax.experimental.pallas import tpu as pltpu
from jax.sharding import PartitionSpec as P

STEP_SIZE = 0.1
SECTION = 4
SIDE = 32
CHANNELS = 128
PIXELS = SIDE * SIDE
PADDED = PIXELS + 2 * SIDE
PIECE = 128
CHUNK = 256
LOW = jnp.bfloat16
FULL = jnp.float32
SENT = jnp.float16

IMAGE = (PIXELS, CHANNELS)
PAD_SCRATCH = (PADDED, 3 * CHANNELS)


def clear(pad):
    edge = jnp.zeros((SIDE, 3 * CHANNELS), LOW)
    pad[0:SIDE, :] = edge
    pad[SIDE + PIXELS : PADDED, :] = edge


def put(pad, piece, values):
    column = lax.broadcasted_iota(jnp.int32, values.shape, 0) % SIDE
    left = jnp.where(column == 0, 0.0, pltpu.roll(values, 1, 0))
    right = jnp.where(column == SIDE - 1, 0.0, pltpu.roll(values, PIECE - 1, 0))
    rows = pl.ds(SIDE + piece * PIECE, PIECE)
    pad[rows, 0:CHANNELS] = left.astype(LOW)
    pad[rows, CHANNELS : 2 * CHANNELS] = values.astype(LOW)
    pad[rows, 2 * CHANNELS : 3 * CHANNELS] = right.astype(LOW)


def put_active(pad, state):
    for piece in range(PIXELS // PIECE):
        put(pad, piece, jnp.tanh(state[pl.ds(piece * PIECE, PIECE), :]))


def conv(pad, kernel, chunk):
    columns = jnp.concatenate(
        [pad[pl.ds(chunk * CHUNK + SIDE * shift, CHUNK), :] for shift in range(3)], axis=1
    )
    return jnp.dot(columns, kernel[...], preferred_element_type=FULL)


def chunks():
    return [(chunk, pl.ds(chunk * CHUNK, CHUNK)) for chunk in range(PIXELS // CHUNK)]


def relax_kernel(begin, weights, out, state, pad):
    clear(pad)
    state[...] = begin[...]

    def step(layer, carry):
        put_active(pad, state)
        for chunk, rows in chunks():
            state[rows, :] += STEP_SIZE * conv(pad, weights.at[layer], chunk)
        return carry

    lax.fori_loop(0, SECTION, step, 0)
    out[...] = state[...]


def fine_kernel(place, own, received, weights, closing, defect_out, first_out, second_out, state, base, first, pad):
    section, phase = place[0], place[1]
    clear(pad)
    for _, rows in chunks():
        begin = jnp.where(section == 0, own[rows, :], received[rows, :])
        state[rows, :] = begin
        base[rows, :] = begin

    put_active(pad, state)
    for chunk, rows in chunks():
        term = conv(pad, weights.at[0], chunk)
        first[rows, :] = term
        state[rows, :] += STEP_SIZE * term

    @pl.when(phase == 0)
    def _():
        for chunk, rows in chunks():
            long_term = (4 * SECTION * STEP_SIZE) * conv(pad, closing.at[SECTION - 1], chunk)
            base[rows, :] += long_term

    def step(layer, carry):
        put_active(pad, state)
        for chunk, rows in chunks():
            state[rows, :] += STEP_SIZE * conv(pad, weights.at[layer], chunk)
        return carry

    lax.fori_loop(1, SECTION, step, 0)
    for _, rows in chunks():
        begin = jnp.where(section == 0, own[rows, :], received[rows, :])
        last = state[rows, :]
        defect = (last - begin) - SECTION * STEP_SIZE * first[rows, :]
        defect_out[rows, :] = defect.astype(LOW)
        first_out[rows, :] = jnp.where(phase == 0, last, defect)
        coarse_part = jnp.where(section == 0, begin, -base[rows, :])
        second_out[rows, :] = jnp.where(phase == 0, coarse_part, defect)


def first_round_kernel(place, mine, coarse_part, near, across, leading, near_out, across_out, state, pad):
    phase = place[1]

    @pl.when(phase < 2)
    def _():
        clear(pad)
        for _, rows in chunks():
            state[rows, :] = jnp.where(phase == 0, mine[rows, :], near[rows, :])
        put_active(pad, state)
        for chunk, rows in chunks():
            defect = jnp.where(phase == 0, near[rows, :], mine[rows, :])
            state[rows, :] += SECTION * STEP_SIZE * conv(pad, leading.at[1], chunk) + defect
            across_out[rows, :] = state[rows, :]
            near_out[rows, :] = coarse_part[rows, :]

    @pl.when(phase == 1)
    def _():
        put_active(pad, state)
        for chunk, rows in chunks():
            change = SECTION * STEP_SIZE * conv(pad, leading.at[2], chunk) + across[rows, :]
            near_out[rows, :] = state[rows, :] + change

    @pl.when(phase >= 2)
    def _():
        for _, rows in chunks():
            near_out[rows, :] = jnp.where(phase == 3, across[rows, :], near[rows, :])
            across_out[rows, :] = near[rows, :]


def closing_kernel(
    place, mine, coarse_part, near, across, level, near_later, across_later, leading, out, base, state, pad
):
    phase, in_first_group = place[1], place[0] < 4
    clear(pad)

    @pl.when(phase < 2)
    def _():
        for _, rows in chunks():
            state[rows, :] = jnp.where(phase == 0, near_later[rows, :], level[rows, :])
            base[rows, :] = jnp.where(phase == 0, coarse_part[rows, :], near_later[rows, :])
            out[rows, :] = jnp.where(phase == 0, across[rows, :], across_later[rows, :])

    @pl.when(phase >= 2)
    def _():
        for _, rows in chunks():
            state[rows, :] = across_later[rows, :]
            base[rows, :] = jnp.where(phase == 2, near_later[rows, :], across[rows, :])
            out[rows, :] = jnp.where(phase == 2, near[rows, :], mine[rows, :])
        put_active(pad, state)
        for chunk, rows in chunks():
            defect = jnp.where(phase == 2, mine[rows, :], near[rows, :])
            state[rows, :] += SECTION * STEP_SIZE * conv(pad, leading.at[2], chunk) + defect

    put_active(pad, state)
    for chunk, rows in chunks():
        closing = state[rows, :] + SECTION * STEP_SIZE * conv(pad, leading.at[3], chunk) + out[rows, :]
        out[rows, :] = closing + jnp.where(in_first_group, 0.0, base[rows, :])


def load(sources, targets, arrived):
    copies = [
        pltpu.make_async_copy(source, target, arrived.at[number])
        for number, (source, target) in enumerate(zip(sources, targets))
    ]
    for copy in copies:
        copy.start()
    return copies


def final_kernel(place, *refs):
    stored, out, refs = refs[:15], refs[15], refs[16:]
    state, begin, end, slopes, change, pads, back_pad, grads, slots = refs[:9]
    held, arrived = refs[9:16], refs[16]
    coarse, images, defects, leading, weights, flipped, end_adjoint = held
    phase, group, replica = place[1], place[2], place[3]
    copies = load(stored, [slots.at[number] for number in range(8)] + list(held), arrived)
    clear(back_pad)
    for layer in range(SECTION):
        clear(pads.at[layer])
    grads[3 * CHANNELS :, :] = jnp.zeros((8, CHANNELS), FULL)

    for copy in copies[:10]:
        copy.wait()
    for _, rows in chunks():
        state[rows, :] = slots[group, rows, :]

    def chain_step(turn, carry):
        put_active(back_pad, state)
        for chunk, rows in chunks():
            long_term = (4 * SECTION * STEP_SIZE) * conv(back_pad, coarse.at[turn], chunk)
            state[rows, :] += long_term + slots[group - turn, rows, :]
        return carry

    lax.fori_loop(1, group, chain_step, 0)
    for _, rows in chunks():
        begin[rows, :] = jnp.where(group == 0, images[rows, :], state[rows, :])

    @pl.when(group > 0)
    def _():
        chain_step(group, 0)

    for _, rows in chunks():
        end[rows, :] = state[rows, :]
        state[rows, :] = begin[rows, :]
    for copy in copies[10:12]:
        copy.wait()

    def level_step(turn, carry):
        put_active(back_pad, state)
        for chunk, rows in chunks():
            state[rows, :] += (
                SECTION * STEP_SIZE * conv(back_pad, leading.at[turn], chunk)
                + defects[turn, rows, :].astype(FULL)
            )

        @pl.when(phase == turn)
        def _():
            end[...] = state[...]

        @pl.when(phase == turn + 1)
        def _():
            begin[...] = state[...]

        return carry

    lax.fori_loop(0, 3, level_step, 0)
    for copy in copies[12:]:
        copy.wait()

    def active(layer):
        for piece in range(PIXELS // PIECE):
            rows = pl.ds(piece * PIECE, PIECE)
            slope = jnp.tanh(begin[rows, :])
            slopes[layer, rows, :] = STEP_SIZE * (1.0 - slope * slope)
            put(pads.at[layer], piece, slope)

    def forward(layer, carry):
        active(layer)
        for chunk, rows in chunks():
            begin[rows, :] += STEP_SIZE * conv(pads.at[layer], weights.at[layer], chunk)
        return carry

    lax.fori_loop(0, SECTION - 1, forward, 0)
    active(SECTION - 1)
    change[...] = jnp.zeros(IMAGE, FULL)

    def backward(turn, carry):
        layer = SECTION - 1 - turn
        for piece in range(PIXELS // PIECE):
            rows = pl.ds(piece * PIECE, PIECE)
            put(back_pad, piece, end_adjoint[rows, :] + change[rows, :])
        low = back_pad[pl.ds(SIDE, PIXELS), CHANNELS : 2 * CHANNELS].T
        for part in range(3):
            offset = 2 * replica + part
            columns = pads[
                layer,
                pl.ds(pl.multiple_of(SIDE * (offset // 3), SIDE), PIXELS),
                pl.ds(pl.multiple_of(CHANNELS * (offset % 3), CHANNELS), CHANNELS),
            ]
            term = jnp.dot(low, columns, preferred_element_type=FULL)
            grads[pl.ds(part * CHANNELS, CHANNELS), :] = STEP_SIZE * term.T
        for block in range(4):
            rows = pl.ds(pl.multiple_of(SIDE * replica + 72 * block, 8), 80)
            out[block, pl.ds(pl.multiple_of(192 + 80 * layer, 16), 80), :] = grads[rows, :].astype(LOW)
        for chunk, rows in chunks():
            change[rows, :] += slopes[layer, rows, :] * conv(back_pad, flipped.at[layer], chunk)
        return carry

    lax.fori_loop(0, SECTION, backward, 0)
    for block in range(4):
        kept = pl.ds(pl.multiple_of(replica * 256 + block * 64, 64), 64)
        high = end[kept, :].astype(LOW)
        out[block, 0:64, :] = high
        out[block, 64:128, :] = (end[kept, :] - high.astype(FULL)).astype(LOW)
        out[block, 128:192, :] = change[kept, :].astype(LOW)


def call(body, outs, scratch, megabytes, place, *operands, stored=()):
    held = pl.BlockSpec(memory_space=pltpu.VMEM)
    in_specs = [held] * len(operands) + [pl.BlockSpec(memory_space=pltpu.HBM)] * len(stored)
    operands += tuple(stored)
    if place is not None:
        in_specs = [pl.BlockSpec(memory_space=pltpu.SMEM)] + in_specs
        operands = (place,) + operands
    return pl.pallas_call(
        body,
        out_shape=outs,
        in_specs=in_specs,
        out_specs=jax.tree.map(lambda _: held, outs),
        scratch_shapes=scratch,
        compiler_params=pltpu.CompilerParams(vmem_limit_bytes=megabytes * 1024 * 1024),
    )(*operands)


def shape(*dims, dtype=FULL):
    return jax.ShapeDtypeStruct(dims, dtype)


def wide():
    return pltpu.VMEM(IMAGE, FULL)


def padding():
    return pltpu.VMEM(PAD_SCRATCH, LOW)


def swap(block, distance, sections):
    moved = lax.ppermute(block.astype(SENT), "layer", [(i, i ^ distance) for i in range(sections)])
    return moved.astype(block.dtype)


def shift(block, distance, sections):
    route = [(i, i + distance) for i in range(sections - distance)]
    return lax.ppermute(block.astype(SENT), "layer", route).astype(block.dtype)


def local(images, end_guess, end_adjoint, weights):
    section = lax.axis_index("layer")
    tile = lax.axis_index("space")
    sections = lax.axis_size("layer")
    tiles = lax.axis_size("space")
    replica = tile // 4
    group = section // 4
    place = jnp.stack([section, section % 4, group, replica]).astype(jnp.int32)
    rows_of_groups = [[4 * g + i for i in range(4)] for g in range(sections // 4)]
    columns_of_groups = [[4 * g + i for g in range(sections // 4)] for i in range(4)]

    guess, leading = lax.optimization_barrier((end_guess[0].astype(SENT), weights[0]))
    leading = lax.all_gather(leading, "layer", axis_index_groups=rows_of_groups)
    guess = jnp.where(section == 0, images, shift(guess, 1, sections).astype(FULL))
    both = jnp.stack([guess, end_adjoint[0]], axis=1).astype(SENT)
    both = lax.all_to_all(jnp.tile(both, (tiles // 4, 1, 1, 1, 1)), "space", 0, 0, tiled=True)
    both = both.astype(FULL)
    start, adjoint_whole = both[:, 0].reshape(IMAGE), both[:, 1].reshape(IMAGE)

    flipped = (
        weights.reshape(SECTION, 9, CHANNELS, CHANNELS)[:, ::-1]
        .transpose(0, 1, 3, 2)
        .reshape(SECTION, 9 * CHANNELS, CHANNELS)
    )
    image_shape = shape(*IMAGE)

    relaxed = call(relax_kernel, image_shape, [wide(), padding()], 8, None, start, weights)
    closing_weights, _ = lax.optimization_barrier((leading[3], relaxed))
    received = shift(relaxed, 1, sections)
    coarse = lax.all_gather(closing_weights, "layer", axis_index_groups=columns_of_groups)
    defect, mine, coarse_part = call(
        fine_kernel,
        (shape(*IMAGE, dtype=LOW), image_shape, image_shape),
        [wide(), wide(), wide(), padding()],
        12, place, start, received, weights, leading,
    )
    defects = lax.all_gather(defect, "layer", axis_index_groups=rows_of_groups)
    near, across = swap(mine, 1, sections), swap(coarse_part, 3, sections)
    level, passed = call(
        first_round_kernel, (image_shape, image_shape), [wide(), padding()], 10,
        place, mine, coarse_part, near, across, leading,
    )
    near_later, across_later = swap(level, 1, sections), swap(passed, 3, sections)
    defect_two, base = call(
        closing_kernel, (image_shape, image_shape), [wide(), padding()], 12,
        place, mine, coarse_part, near, across, level, near_later, across_later, leading,
    )
    up = [(i, (i + 4) % sections) for i in range(sections)]
    down = [(j, i) for i, j in up]
    def ring(route, turns):
        block, wide_blocks = lax.ppermute(defect_two.astype(SENT), "layer", route), []
        for _ in range(turns - 1):
            moved, ready = lax.optimization_barrier((lax.ppermute(block, "layer", route), block.astype(FULL)))
            wide_blocks.append(ready)
            block = moved
        return block, wide_blocks

    farthest, ups = ring(up, 4)
    last_down, downs = ring(down, 3)
    farthest, last_down = lax.optimization_barrier((farthest, last_down.astype(FULL)))
    downs.append(last_down)

    farthest, coarse = lax.optimization_barrier((farthest, coarse))
    slots = [defect_two, *ups, farthest.astype(FULL), *downs[::-1]]
    stored = (coarse, base, defects, leading, weights, flipped, adjoint_whole)
    parts = call(
        final_kernel,
        shape(4, 512, CHANNELS, dtype=LOW),
        [
            wide(), wide(), wide(),
            pltpu.VMEM((SECTION, *IMAGE), FULL),
            wide(),
            pltpu.VMEM((SECTION, *PAD_SCRATCH), LOW),
            padding(),
            pltpu.VMEM((3 * CHANNELS + 8, CHANNELS), FULL),
            pltpu.VMEM((8, *IMAGE), FULL),
            *[pltpu.VMEM(array.shape, array.dtype) for array in stored],
            pltpu.SemaphoreType.DMA((8 + len(stored),)),
        ],
        60, place, stored=(*slots, *stored),
    )
    row_groups = [[4 * r + n for n in range(4)] for r in range(tiles // 4)]
    parts = lax.all_to_all(parts, "space", 0, 0, axis_index_groups=row_groups, tiled=True).astype(FULL)
    tile_shape = (1, 4, 2, SIDE, CHANNELS)
    section_ends = (parts[:, 0:64] + parts[:, 64:128]).reshape(tile_shape)
    start_adjoint = end_adjoint + parts[:, 128:192].reshape(tile_shape)
    weight_grad = parts[:, 192:].sum(0).reshape(SECTION, 80, CHANNELS)[:, :72]
    return section_ends, start_adjoint, weight_grad


def solution(mesh):
    return jax.shard_map(
        local,
        mesh=mesh,
        in_specs=(
            P(None, "space", None, None),
            P("layer", None, "space", None, None),
            P("layer", None, "space", None, None),
            P("layer", None, None),
        ),
        out_specs=(
            P("layer", None, "space", None, None),
            P("layer", None, "space", None, None),
            P("layer", "space", None),
        ),
        check_vma=False,
    )
```
